256 devices in a mesh: ctx: 16 (over z, core), head: 16 (over x, y).
Axes of the slice: x: 4, y: 4, z: 8, core: 2. Of those that a mesh axis runs over, the one named last changes fastest.
Arguments:
- query_states: bfloat16 [8192, 8192], P('ctx', 'head'), may hold values from -8 to 8
- key_states: bfloat16 [8192, 1024], P('ctx'), may hold values from -8 to 8
- value_states: bfloat16 [8192, 1024], P('ctx'), may hold values from -6 to 6
- out_grad: bfloat16 [8192, 8192], P('ctx', 'head'), may hold values from -6 to 6
- stretch_order: int32 [64], replicated, may hold values from 0 to 63, each once
- doc_blocks: int32 [16], replicated, may hold values from 1 to 8, 64 in all
Outputs:
- attention_out: bfloat16 [8192, 8192], P('ctx', 'head')
- query_grad: bfloat16 [8192, 8192], P(('ctx', 'head'))
- key_grad: bfloat16 [8192, 1024], P(('ctx', 'head'))
- value_grad: bfloat16 [8192, 1024], P(('ctx', 'head'))
The draws below stay inside these ranges and needn't reach their ends.
Inputs may be any that keep to these rules, and one draw needn't show every extreme that they name: `doc_blocks`: each document spans 1 to 8 stretches.
All inputs are finite; a program needn't handle non-finite values.
Results may differ from the reference program's by a relative error of at most 0.035.
Values may be sent and summed in bfloat16 or wider, within the bound.
A program may use at most 128 MiB of HBM per device.

```python
import math
import jax
import jax.numpy as jnp
import numpy as np
from jax import lax

QHEADS = 64
KVHEADS = 8
HD = 128
STRETCH = 128
NBLK = 64
SEQ = 8192
MOSTDOC = 8
NDOC = 16


def draw_query_states(key, part):
    drawn = jax.random.normal(jax.random.fold_in(key, 101), (SEQ, QHEADS * HD), jnp.float32)
    return jnp.clip(drawn, -6.0, 6.0).astype(jnp.bfloat16)


def draw_key_states(key, part):
    drawn = jax.random.normal(jax.random.fold_in(key, 102), (SEQ, KVHEADS * HD), jnp.float32)
    return jnp.clip(drawn, -6.0, 6.0).astype(jnp.bfloat16)


def steps_of(stream_key, shape, split, low, high):
    factor_of, own = 1.0, jax.random.fold_in(stream_key, 6)
    for dim, shards_of in split:
        heights = jnp.exp(jax.random.uniform(jax.random.fold_in(own, dim), (shards_of,), jnp.float32, low / len(split), high / len(split)))
        factor_of = factor_of * jnp.repeat(heights, shape[dim] // shards_of).reshape([-1 if axis == dim else 1 for axis in range(len(shape))])
    return factor_of


def split_up(number_of, total, reach, slope):
    weights = [(1 << 20) // math.isqrt(standing ** slope) + 1 for standing in range(2, number_of + 1)]
    surplus, holding = total - reach - (number_of - 1), [1] * (number_of - 1)
    while surplus > 0:
        movable = [i for i in range(number_of - 1) if holding[i] < reach]
        mass, left = sum([weights[i] for i in movable]), surplus
        for i in movable:
            more = min(reach - holding[i], max(1, left * weights[i] // mass), surplus)
            holding[i] = holding[i] + more
            surplus = surplus - more
    return np.array([reach] + holding)


def uneven(stream_key, count, total, limit, slope):
    if count == 2:
        one = jax.random.randint(stream_key, (), max(1, total - limit), min(limit, total - 1) + 1)
        return jnp.stack([one, total - one])
    lengths = jnp.asarray(split_up(count, total, limit, slope), jnp.int32)
    pairs = (count - 1) // 2
    giver, receiver = lengths[1:1 + 2 * pairs:2], lengths[2:2 + 2 * pairs:2]
    slack = jnp.minimum(giver - 1, limit - receiver)
    moved = jax.random.randint(jax.random.fold_in(stream_key, 1), (pairs,), 0, 1 << 20) % (slack + 1)
    lengths = lengths.at[1:1 + 2 * pairs:2].set(giver - moved).at[2:2 + 2 * pairs:2].set(receiver + moved)
    return lengths[jax.random.permutation(jax.random.fold_in(stream_key, 2), count)]


def centred(key, dims, scale, bound, cuts=(), held_as=jnp.bfloat16):
    factor_of = steps_of(key, dims, cuts, -0.22, 0.18) if cuts else 1.0
    result = jax.random.normal(key, dims, jnp.float32) * scale * factor_of
    return jnp.minimum(jnp.maximum(result, -bound), bound).astype(held_as)


def setup_inputs(seed: int = 0) -> dict:
    keys = jax.random.split(jax.random.key(seed), 7)
    return {
        "query_states": draw_query_states(jax.random.fold_in(keys[6], 71), 0),
        "key_states": draw_key_states(jax.random.fold_in(keys[6], 71), 0),
        "value_states": centred(keys[2], (SEQ, KVHEADS * HD), 1.0, 6.0, ((0, 16),)),
        "out_grad": centred(keys[3], (SEQ, QHEADS * HD), 1.0, 6.0, ((0, 16), (1, 16))),
        "stretch_order": jax.random.permutation(keys[4], NBLK).astype(jnp.int32),
        "doc_blocks": uneven(keys[5], NDOC, NBLK, MOSTDOC, 2).astype(jnp.int32),
    }


def reference(query_states, key_states, value_states, out_grad, stretch_order, doc_blocks):
    group_size = QHEADS // KVHEADS
    scale_factor = HD ** -0.5
    largest_score = lax.Precision.HIGHEST
    table = jnp.arange(NBLK, dtype=jnp.int32)
    slot_lookup = jnp.sum(jnp.where(stretch_order[None, :] == table[:, None], table[None, :], 0), axis=1).astype(jnp.int32)
    within = jnp.arange(STRETCH, dtype=jnp.int32)
    offsets = jnp.arange(MOSTDOC, dtype=jnp.int32)
    reach_stretch = table[:, None] - MOSTDOC + 1 + offsets[None, :]
    reach_valid = reach_stretch >= 0
    reach_clamp = jnp.maximum(reach_stretch, 0).astype(jnp.int32)
    query_pos = table[:, None] * STRETCH + within[None, :]
    key_pos = (reach_stretch[:, :, None] * STRETCH + within[None, None, :]).reshape(NBLK, MOSTDOC * STRETCH)
    key_valid = jnp.broadcast_to(reach_valid[:, :, None], (NBLK, MOSTDOC, STRETCH)).reshape(NBLK, MOSTDOC * STRETCH)
    doc_ends = jnp.cumsum(doc_blocks) * STRETCH

    def doc_numbers(positions):
        return jnp.sum((positions[..., None] >= doc_ends).astype(jnp.int32), axis=-1)

    allowed = (doc_numbers(query_pos)[:, :, None] == doc_numbers(key_pos)[:, None, :]) & (key_pos[:, None, :] <= query_pos[:, :, None]) & key_valid[:, None, :]

    def to_window(array):
        return array.reshape(NBLK, STRETCH, array.shape[1])[slot_lookup]

    query_w = to_window(query_states)
    key_w = to_window(key_states)
    value_w = to_window(value_states)
    grad_w = to_window(out_grad)

    def one_group(kv_number):
        key_one = lax.dynamic_slice_in_dim(key_w, kv_number * HD, HD, 2).astype(jnp.float32)
        value_one = lax.dynamic_slice_in_dim(value_w, kv_number * HD, HD, 2).astype(jnp.float32)
        key_extent = key_one[reach_clamp].reshape(NBLK, MOSTDOC * STRETCH, HD)
        value_extent = value_one[reach_clamp].reshape(NBLK, MOSTDOC * STRETCH, HD)
        key_total = jnp.zeros((NBLK, STRETCH, HD), jnp.float32)
        value_total = jnp.zeros((NBLK, STRETCH, HD), jnp.float32)
        attention_list = []
        query_list = []
        for member in range(group_size):
            head_number = kv_number * group_size + member
            query_single = lax.dynamic_slice_in_dim(query_w, head_number * HD, HD, 2).astype(jnp.float32)
            gradient_single = lax.dynamic_slice_in_dim(grad_w, head_number * HD, HD, 2).astype(jnp.float32)
            logit_scores = jnp.einsum("wcn,wzn->wcz", query_single, key_extent, precision=largest_score) * scale_factor
            logit_scores = jnp.where(allowed, logit_scores, -1.0e30)
            row_max = jnp.max(logit_scores, axis=2)
            totals = jnp.sum(jnp.where(allowed, jnp.exp(logit_scores - row_max[..., None]), 0.0), axis=2)
            log_total = row_max + jnp.log(totals)
            weights = jnp.where(allowed, jnp.exp(logit_scores - log_total[..., None]), 0.0)
            weights_blocked = weights.astype(jnp.bfloat16).astype(jnp.float32)
            attention_single = jnp.einsum("rpl,rlo->rpo", weights_blocked, value_extent, precision=largest_score).astype(jnp.bfloat16)
            row_dots = jnp.sum(gradient_single * attention_single.astype(jnp.float32), axis=2)
            weight_gradient = jnp.einsum("wcn,wzn->wcz", gradient_single, value_extent, precision=largest_score)
            score_gradient = (weights * (weight_gradient - row_dots[..., None])).astype(jnp.bfloat16).astype(jnp.float32)
            query_portion = (jnp.einsum("rpl,rlo->rpo", score_gradient, key_extent, precision=largest_score) * scale_factor).astype(jnp.bfloat16)
            key_portion = jnp.einsum("rin,rih->rnh", score_gradient, query_single, precision=largest_score)
            value_portion = jnp.einsum("rin,rih->rnh", weights_blocked, gradient_single, precision=largest_score)
            key_total = key_total.at[reach_clamp.reshape(-1)].add(key_portion.reshape(NBLK * MOSTDOC, STRETCH, HD))
            value_total = value_total.at[reach_clamp.reshape(-1)].add(value_portion.reshape(NBLK * MOSTDOC, STRETCH, HD))
            attention_list.append(attention_single)
            query_list.append(query_portion)
        return jnp.stack(attention_list), jnp.stack(query_list), key_total * scale_factor, value_total

    attention_parts, query_parts, key_parts, value_parts = lax.map(one_group, jnp.arange(KVHEADS, dtype=jnp.int32))
    attention_parts = attention_parts.reshape(QHEADS, NBLK, STRETCH, HD)[:, stretch_order]
    query_parts = query_parts.reshape(QHEADS, NBLK, STRETCH, HD)[:, stretch_order]
    attention_out = attention_parts.transpose(1, 2, 0, 3).reshape(SEQ, QHEADS * HD)
    query_grad = query_parts.transpose(1, 2, 0, 3).reshape(SEQ, QHEADS * HD)
    key_grad = key_parts[:, stretch_order].transpose(1, 2, 0, 3).reshape(SEQ, KVHEADS * HD).astype(jnp.bfloat16)
    value_grad = value_parts[:, stretch_order].transpose(1, 2, 0, 3).reshape(SEQ, KVHEADS * HD).astype(jnp.bfloat16)
    return (attention_out, query_grad, key_grad, value_grad)
```

```python
import functools

import jax
import jax.numpy as jnp
from jax import lax
from jax.experimental import pallas as pl
from jax.experimental.pallas import tpu as pltpu
from jax.sharding import PartitionSpec as P

HD = 128
STRETCH = 128
REACH = 8
MASKED = -1e30
XROWS = 128
LOG2E = 1.4426950408889634

AG_UPX, AG_UPC, AG_DNC, AG_DNX, AG_YU, AG_YD, AG_SR, AG_SO, AG_N = 0, 4, 7, 11, 14, 18, 21, 29, 37
RS_S, RS_Y, RS_UPX, RS_UPC, RS_DNC, RS_DNX, RS_N = 0, 8, 16, 20, 24, 28, 32


def when(cond, fn):
    if isinstance(cond, bool):
        if cond:
            fn()
    else:
        pl.when(cond)(fn)


def rows(start, size, unit=32):
    return pl.ds(pl.multiple_of(start, unit), size)


def kernel(
    nz, nh,
    order, blocks, q_hbm, k_hbm, v_hbm, g_hbm,
    out_hbm, dq_ref, dk_ref, dv_ref,
    kbuf, vbuf, qcat, gcat, kext, kt, st, wbuf, dst, contrib_v, contrib_k,
    part_v, part_k, sib_v, sib_k, ysend, yrecv, ux, uc, dc, dx, sux, suc, sdc, sdx,
    fin, finrecv, outbuf, dqbuf, dqrecv, slots, bias,
    ag_recv, ag_send, rs_recv, rs_send, fin_recv, fin_send, dq_recv, dq_send, load_sem, out_sem,
):
    ctx = lax.axis_index("ctx")
    head = lax.axis_index("head")
    z, core = ctx // 2, lax.rem(ctx, 2)
    par = lax.rem(head, 2)
    group = head // 2
    local = 4 * STRETCH
    crows = local - 2 * XROWS
    ring_rows = XROWS + crows
    x0, ox0, ring0 = par * 3, 3 - par * 3, par
    far = nz // 2
    short = local // nh
    scale = HD ** (-0.5)

    def zmod(v):
        return lax.rem(v + nz, nz)

    up = {"ctx": zmod(z + 1) * 2 + core}
    down = {"ctx": zmod(z - 1) * 2 + core}
    sib = {"ctx": z * 2 + 1 - core}
    partner = {"head": head + 1 - 2 * par}

    gathered = (kbuf, vbuf)

    def load_kv(t):
        src = (k_hbm, v_hbm)[t].at[:, pl.ds(pl.multiple_of(group * HD, HD), HD)]
        return [
            pltpu.make_async_copy(
                src.at[pl.ds(i * STRETCH, STRETCH)], gathered[t].at[ctx * 4 + i], load_sem.at[t, i]
            )
            for i in range(4)
        ]

    for t in range(2):
        for copy in load_kv(t):
            copy.start()

    def load_qg(n, s, h):
        src, dst_ = ((q_hbm, qcat), (g_hbm, gcat))[n]
        return pltpu.make_async_copy(
            src.at[pl.ds(s * STRETCH, STRETCH), pl.ds(h * HD, HD)],
            dst_.at[s, pl.ds(h * STRETCH, STRETCH)],
            load_sem.at[2 + n, s * 4 + h],
        )

    heads = [(n, s, h) for n in range(2) for s in range(4) for h in range(4)]
    for n, s, h in heads:
        load_qg(n, s, h).start()

    barrier = pltpu.get_barrier_semaphore()
    for who in (up, down, sib):
        pl.semaphore_signal(barrier, inc=1, device_id=who, device_id_type=pl.DeviceIdType.MESH)
    for i in range(1, nh):
        pl.semaphore_signal(
            barrier, inc=1, device_id={"head": lax.rem(head + i, nh)},
            device_id_type=pl.DeviceIdType.MESH,
        )

    zero_row = jnp.zeros((STRETCH, HD), jnp.float32)
    contrib_v[4 * REACH] = zero_row
    contrib_k[4 * REACH] = zero_row
    for t in range(2):
        ux[t, 0] = jnp.zeros((XROWS, HD), jnp.bfloat16)
        dc[t, 0] = jnp.zeros((2, STRETCH, HD), jnp.bfloat16)
        uc[t, 1] = jnp.zeros((2, STRETCH, HD), jnp.bfloat16)
        dx[t, 1] = jnp.zeros((XROWS, HD), jnp.bfloat16)
    first_b = XROWS // short
    last_b = (local - XROWS) // short

    def fill(p):
        for t in range(2):
            for i in range(nh // 2):
                finrecv[t, 2 * i + p] = jnp.zeros((short, HD), jnp.bfloat16)

    pl.when(head >= last_b)(lambda: fill(0))
    pl.when(head < first_b)(lambda: fill(1))

    pl.semaphore_wait(barrier, nh + 2)

    def piece(t, z_of, core_of, start, size):
        return gathered[t].at[pl.ds((z_of * 2 + core_of) * 4 + start, size)]

    def ag_copy(t, z_of, start, size, sem, device):
        ref = piece(t, z_of, core, start, size)
        return pltpu.make_async_remote_copy(
            src_ref=ref, dst_ref=ref, send_sem=ag_send.at[t, sem], recv_sem=ag_recv.at[t, sem],
            device_id=device, device_id_type=pl.DeviceIdType.MESH,
        )

    def ag_wait(t, z_of, core_of, start, size, sem):
        ref = piece(t, z_of, core_of, start, size)
        pltpu.make_async_remote_copy(
            src_ref=ref, dst_ref=ref, send_sem=ag_send.at[t, sem], recv_sem=ag_recv.at[t, sem],
            device_id=up, device_id_type=pl.DeviceIdType.MESH,
        ).wait_recv()

    def ag_first(t):
        for copy in load_kv(t):
            copy.wait()
        ag_copy(t, z, x0, 1, AG_UPX, up).start()
        ag_copy(t, z, 1, 2, AG_DNC, down).start()
        ag_copy(t, z, 1, 2, AG_UPC, up).start()
        ag_copy(t, z, x0, 1, AG_DNX, down).start()
        ag_copy(t, z, ring0, 3, AG_SR, sib).start()
        ag_copy(t, z, ox0, 1, AG_SO, sib).start()

    def ag_partner(t, k):
        zo = zmod(z - k)
        ag_wait(t, zo, core, ox0, 1, AG_YU + k - 1)
        ag_copy(t, zo, ox0, 1, AG_SO + k, sib).start()

        def lower():
            zd = zmod(z + k)
            ag_wait(t, zd, core, ox0, 1, AG_YD + k - 1)
            ag_copy(t, zd, ox0, 1, AG_SO + nz - k, sib).start()

        when(k < far, lower)

    def ag_step(t, k):
        zo, zd = zmod(z - k), zmod(z + k)
        ag_wait(t, zo, core, x0, 1, AG_UPX + k - 1)
        when(k < far, lambda: ag_copy(t, zo, x0, 1, AG_UPX + k, up).start())
        ag_copy(t, zo, x0, 1, AG_YU + k - 1, partner).start()
        ag_wait(t, zd, core, 1, 2, AG_DNC + k - 1)
        when(k < far, lambda: ag_copy(t, zd, 1, 2, AG_DNC + k, down).start())

        def near():
            ag_wait(t, zo, core, 1, 2, AG_UPC + k - 1)
            when(k < far - 1, lambda: ag_copy(t, zo, 1, 2, AG_UPC + k, up).start())
            ag_wait(t, zd, core, x0, 1, AG_DNX + k - 1)
            when(k < far - 1, lambda: ag_copy(t, zd, x0, 1, AG_DNX + k, down).start())
            ag_copy(t, zd, x0, 1, AG_YD + k - 1, partner).start()
            ag_copy(t, zd, ring0, 3, AG_SR + nz - k, sib).start()

        when(k < far, near)
        ag_copy(t, zo, ring0, 3, AG_SR + k, sib).start()
        when(k > 1, lambda: ag_partner(t, k - 1))

    def ag_finish(t):
        ag_partner(t, far)

        @pl.loop(0, nz)
        def _(d):
            zo = zmod(z - d)
            ag_wait(t, zo, 1 - core, ring0, 3, AG_SR + d)
            ag_wait(t, zo, 1 - core, ox0, 1, AG_SO + d)

    def tables():
        total = order.shape[0]
        for s in range(4):
            own = order[ctx * 4 + s]

            def seek(i, found):
                here = order[i]
                return tuple(
                    jnp.where(here == own - (REACH - 1) + j, i, found[j]) for j in range(REACH)
                )

            found = lax.fori_loop(0, total, seek, (jnp.int32(0),) * REACH)

            def begin(i, carry):
                end, start = carry
                end = end + blocks[i]
                return end, jnp.where(end <= own, end, start)

            _, start = lax.fori_loop(
                0, blocks.shape[0], begin, (jnp.int32(0), jnp.int32(0))
            )
            for j in range(REACH):
                slots[s * REACH + j] = found[j]
                bias[s * REACH + j] = jnp.where(
                    own - (REACH - 1) + j >= start, jnp.float32(0.0), jnp.float32(MASKED)
                )

    nt = (((1,), (1,)), ((), ()))
    nn = (((1,), (0,)), ((), ()))

    def dot(a, b, dims):
        return lax.dot_general(a, b, dims, preferred_element_type=jnp.float32)

    def block(j):
        return pl.ds(pl.multiple_of(j * STRETCH, STRETCH), STRETCH)

    def extent(t, s):
        for j in range(REACH):
            value = gathered[t][slots[s * REACH + j]]
            kext[pl.ds(j * STRETCH, STRETCH), :] = value
            kt[:, pl.ds(j * STRETCH, STRETCH)] = value.T

    def fold(value, op):
        return op(value.reshape(STRETCH // 8, 8, value.shape[1]), axis=0)

    def forward(s):
        q = qcat[s]
        for j in range(REACH):
            kext[pl.ds(j * STRETCH, STRETCH), :] = kbuf[slots[s * REACH + j]]
        st[...] = dot(kext[...], q, nt)
        key_at = lax.broadcasted_iota(jnp.int32, (STRETCH, STRETCH), 0)
        query_at = lax.broadcasted_iota(jnp.int32, (STRETCH, STRETCH), 1)
        causal = key_at <= query_at
        diag = pl.ds((REACH - 1) * STRETCH, STRETCH)
        raw = st[diag, :] * (scale * LOG2E)
        raw = jnp.concatenate(
            [jnp.where(causal, raw[:, h * HD:(h + 1) * HD], MASKED) for h in range(4)], axis=1
        )
        st[diag, :] = raw

        def highest(j, top):
            value = st[block(j), :] * (scale * LOG2E) + bias[s * REACH + j]
            st[block(j), :] = value
            return jnp.maximum(top, fold(value, jnp.max))

        top = lax.fori_loop(0, REACH - 1, highest, fold(raw, jnp.max))
        top = jnp.max(top, axis=0, keepdims=True)

        def exps(j, total):
            value = jnp.exp2(st[block(j), :] - top)
            st[block(j), :] = value
            return total + fold(value, jnp.sum)

        total = lax.fori_loop(0, REACH, exps, jnp.zeros((8, 512), jnp.float32))
        inverse = 1.0 / jnp.sum(total, axis=0, keepdims=True)

        @pl.loop(0, REACH)
        def _(j):
            wbuf[s, block(j), :] = (
                st[block(j), :] * inverse
            ).astype(jnp.bfloat16)

        contrib_v[pl.ds(s * REACH, REACH)] = dot(
            wbuf[s], gcat[s], nn
        ).reshape(REACH, STRETCH, HD)

    per = STRETCH // short

    def backward(s):
        g = gcat[s]
        extent(1, s)
        st[...] = dot(kext[...], g, nt)
        ot = dot(kt[...], wbuf[s], nn).astype(jnp.bfloat16)
        ot = ot.astype(jnp.float32)
        dots = []
        for h in range(4):
            part = ot[:, h * HD:(h + 1) * HD]
            outbuf[s, :, pl.ds(h * HD, HD)] = part.T.astype(jnp.bfloat16)
            gt = g[h * STRETCH:(h + 1) * STRETCH, :].astype(jnp.float32).T
            dots.append(jnp.sum(gt * part, axis=0, keepdims=True))
        dots = jnp.concatenate(dots, axis=1)
        pltpu.make_async_copy(
            outbuf.at[s],
            out_hbm.at[rows(s * STRETCH, STRETCH, STRETCH)], out_sem.at[s],
        ).start()

        @pl.loop(0, REACH)
        def _(j):
            w = wbuf[s, block(j), :].astype(jnp.float32)
            dst[block(j), :] = (w * (st[block(j), :] - dots)).astype(jnp.bfloat16)

        contrib_k[pl.ds(s * REACH, REACH)] = (
            dot(dst[...], qcat[s], nn) * scale
        ).reshape(REACH, STRETCH, HD)
        extent(0, s)
        dqt = dot(kt[...], dst[...], nn) * scale
        for h in range(4):
            dqbuf[pl.ds(s * per, per), :, pl.ds(h * HD, HD)] = dqt[
                :, h * HD:(h + 1) * HD
            ].T.reshape(per, short, HD).astype(jnp.bfloat16)

        @pl.loop(0, per)
        def _(i):
            b = s * per + i

            def remote():
                dq_copy(b, head, b).start()

            def own():
                dqrecv[head] = dqbuf[b]

            pl.when(b != head)(remote)
            pl.when(b == head)(own)

    def dq_copy(b, src, to):
        return pltpu.make_async_remote_copy(
            src_ref=dqbuf.at[b], dst_ref=dqrecv.at[src],
            send_sem=dq_send.at[b], recv_sem=dq_recv.at[src],
            device_id={"head": to}, device_id_type=pl.DeviceIdType.MESH,
        )

    contribs = (contrib_k, contrib_v)
    parts = (part_k, part_v)
    sibs = (sib_k, sib_v)

    def build(t, at):
        for k in range(4):
            here = order[at * 4 + k]
            total = None
            for s in range(4):
                delta = order[ctx * 4 + s] - here
                index = jnp.where(
                    (delta >= 0) & (delta < REACH), s * REACH + REACH - 1 - delta, 4 * REACH
                )
                term = contribs[t][index]
                total = term if total is None else total + term
            parts[t][at * 4 + k] = total.astype(jnp.bfloat16)

    def rs_copy(t, src, dst_, sem, device):
        return pltpu.make_async_remote_copy(
            src_ref=src, dst_ref=dst_, send_sem=rs_send.at[t, sem], recv_sem=rs_recv.at[t, sem],
            device_id=device, device_id_type=pl.DeviceIdType.MESH,
        )

    def rs_wait(t, ref, sem):
        rs_copy(t, ref, ref, sem, up).wait_recv()

    def dest(i):
        return zmod(z + far + ((i + 1) // 2) * (2 * lax.rem(i, 2) - 1))

    def rs_build(t):
        @pl.loop(0, nz)
        def _(i):
            zt = dest(i)
            other = zt * 2 + 1 - core
            build(t, other)
            rs_copy(
                t, parts[t].at[pl.ds(other * 4, 4)], sibs[t].at[pl.ds(i * 4, 4)], RS_S + i, sib
            ).start()
            build(t, zt * 2 + core)

    def place(i):
        if i == nz - 1:
            return z
        delta = far + ((i + 1) // 2) * (2 * (i % 2) - 1)
        return zmod(z + delta)

    def chip_sum(t, i, start, size):
        return (
            parts[t][pl.ds((place(i) * 2 + core) * 4 + start, size)].astype(jnp.float32)
            + sibs[t][pl.ds(i * 4 + start, size)].astype(jnp.float32)
        )

    def rs_partner(t):
        for i in range(nz):
            rs_wait(t, sibs[t].at[pl.ds(i * 4, 4)], RS_S + i)
            ysend[t, i] = chip_sum(t, i, ox0, 1)[0].astype(jnp.bfloat16)
            rs_copy(t, ysend.at[t, i], yrecv.at[t, i], RS_Y + i, partner).start()

    def own_x(t, i):
        rs_wait(t, yrecv.at[t, i], RS_Y + i)
        return chip_sum(t, i, x0, 1)[0] + yrecv[t, i].astype(jnp.float32)

    def own_c(t, i):
        return chip_sum(t, i, 1, 2)

    def rs_step(t, k):
        iu, idn = 2 * (k - 1), max(0, 2 * k - 3)
        when(k > 1, lambda: rs_wait(t, ux.at[t, k - 1], RS_UPX + k - 2))
        sux[t, k] = (own_x(t, iu) + ux[t, k - 1].astype(jnp.float32)).astype(jnp.bfloat16)
        rs_copy(t, sux.at[t, k], ux.at[t, k], RS_UPX + k - 1, up).start()
        when(k > 1, lambda: rs_wait(t, dc.at[t, k - 1], RS_DNC + k - 2))
        sdc[t, k] = (own_c(t, idn) + dc[t, k - 1].astype(jnp.float32)).astype(jnp.bfloat16)
        rs_copy(t, sdc.at[t, k], dc.at[t, k], RS_DNC + k - 1, down).start()

        def near():
            when(k > 2, lambda: rs_wait(t, uc.at[t, k - 1], RS_UPC + k - 2))
            suc[t, k] = (own_c(t, iu) + uc[t, k - 1].astype(jnp.float32)).astype(jnp.bfloat16)
            rs_copy(t, suc.at[t, k], uc.at[t, k], RS_UPC + k - 1, up).start()
            when(k > 2, lambda: rs_wait(t, dx.at[t, k - 1], RS_DNX + k - 2))
            sdx[t, k] = (own_x(t, idn) + dx[t, k - 1].astype(jnp.float32)).astype(jnp.bfloat16)
            rs_copy(t, sdx.at[t, k], dx.at[t, k], RS_DNX + k - 1, down).start()

        when(k > 1, near)

    b0 = par * (XROWS // short)
    nb = ring_rows // short
    own_in = (head >= b0) & (head < b0 + nb)

    def fin_copy(t, b, src):
        return pltpu.make_async_remote_copy(
            src_ref=fin.at[t, rows(b * short, short)], dst_ref=finrecv.at[t, src],
            send_sem=fin_send.at[t, b], recv_sem=fin_recv.at[t, src],
            device_id={"head": b}, device_id_type=pl.DeviceIdType.MESH,
        )

    def rs_final(t):
        rs_wait(t, ux.at[t, far], RS_UPX + far - 1)
        rs_wait(t, dx.at[t, far], RS_DNX + far - 1)
        fin[t, rows(x0 * STRETCH, XROWS), :] = (
            own_x(t, nz - 1) + ux[t, far].astype(jnp.float32) + dx[t, far].astype(jnp.float32)
        ).astype(jnp.bfloat16)
        rs_wait(t, uc.at[t, far], RS_UPC + far - 1)
        rs_wait(t, dc.at[t, far], RS_DNC + far - 1)
        fin[t, pl.ds(XROWS, crows), :] = (
            own_c(t, nz - 1) + uc[t, far].astype(jnp.float32) + dc[t, far].astype(jnp.float32)
        ).reshape(crows, HD).astype(jnp.bfloat16)

        @pl.loop(0, nb)
        def _(i):
            b = b0 + i
            pl.when(b != head)(lambda: fin_copy(t, b, head).start())

            def keep():
                finrecv[t, head] = fin[t, rows(head * short, short), :]

            pl.when(b == head)(keep)

    def rs_out(t, ref):
        @pl.loop(0, nh)
        def _(src):
            p = lax.rem(src, 2)
            sends = ((p == 0) & (head < last_b)) | ((p == 1) & (head >= first_b))
            pl.when(sends & (src != head))(lambda: fin_copy(t, 0, src).wait_recv())

        for g in range(nh // 2):
            ref[:, g * HD:(g + 1) * HD] = (
                finrecv[t, 2 * g].astype(jnp.float32) + finrecv[t, 2 * g + 1].astype(jnp.float32)
            ).astype(jnp.bfloat16)

    ag_first(0)
    tables()

    @pl.loop(1, far)
    def _(k):
        ag_step(0, k)

    ag_first(1)
    ag_step(0, far)
    ag_finish(0)
    for n, s, h in heads:
        load_qg(n, s, h).wait()
    ag_step(1, 1)

    @pl.loop(0, 4)
    def _(s):
        forward(s)
        pl.when(s < far - 1)(lambda: ag_step(1, s + 2))

    ag_finish(1)
    rs_build(1)
    rs_partner(1)
    rs_step(1, 1)

    for s in range(4):
        backward(s)
        if s < far - 1:
            rs_step(1, s + 2)

    rs_build(0)
    rs_partner(0)
    rs_step(0, 1)
    rs_final(1)

    for k in range(2, far + 1):
        rs_step(0, k)

    rs_out(1, dv_ref)
    rs_final(0)
    rs_out(0, dk_ref)

    @pl.loop(0, nh)
    def _(src):
        pl.when(src != head)(lambda: dq_copy(0, src, src).wait_recv())

    for src in range(nh):
        dq_ref[:, src * 4 * HD:(src + 1) * 4 * HD] = dqrecv[src]
    @pl.loop(0, nh)
    def _(b):
        pl.when(b != head)(lambda: dq_copy(b, head, b).wait_send())

    for s in range(4):
        pltpu.make_async_copy(
            outbuf.at[s], out_hbm.at[pl.ds(s * STRETCH, STRETCH)], out_sem.at[s]
        ).wait()
    for t in range(2):
        for first, count, size in (
            (AG_UPX, far, 1), (AG_UPC, far - 1, 2), (AG_DNC, far, 2), (AG_DNX, far - 1, 1),
            (AG_YU, far, 1), (AG_YD, far - 1, 1), (AG_SR, nz, 3), (AG_SO, nz, 1),
        ):

            @pl.loop(first, first + count)
            def _(sem):
                ag_copy(t, z, 0, size, sem, up).wait_send()

        for first, count, ref in (
            (RS_S, nz, sibs[t].at[pl.ds(0, 4)]), (RS_Y, nz, yrecv.at[t, 0]),
            (RS_UPX, far, ux.at[t, 0]), (RS_UPC + 1, far - 1, uc.at[t, 0]),
            (RS_DNC, far, dc.at[t, 0]), (RS_DNX + 1, far - 1, dx.at[t, 0]),
        ):

            @pl.loop(first, first + count)
            def _(sem):
                rs_copy(t, ref, ref, sem, up).wait_send()

        @pl.loop(0, nb)
        def _(i):
            pl.when(b0 + i != head)(lambda: fin_copy(t, b0 + i, head).wait_send())


def on_device(query_states, key_states, value_states, out_grad, stretch_order, doc_blocks):
    nz = lax.axis_size("ctx") // 2
    nh = lax.axis_size("head")
    far = nz // 2
    local = 4 * STRETCH
    crows = local - 2 * XROWS
    short = local // nh
    seq = 2 * nz * local
    bf, f32 = jnp.bfloat16, jnp.float32
    anywhere = pl.BlockSpec(memory_space=pl.ANY)
    smem = pl.BlockSpec(memory_space=pltpu.SMEM)
    vmem = pl.BlockSpec(memory_space=pltpu.VMEM)
    V, D = pltpu.VMEM, pltpu.SemaphoreType.DMA
    return pl.pallas_call(
        functools.partial(kernel, nz, nh),
        out_shape=(
            jax.ShapeDtypeStruct((local, 4 * HD), bf),
            jax.ShapeDtypeStruct((short, nh * 4 * HD), bf),
            jax.ShapeDtypeStruct((short, nh // 2 * HD), bf),
            jax.ShapeDtypeStruct((short, nh // 2 * HD), bf),
        ),
        in_specs=[smem, smem, anywhere, anywhere, anywhere, anywhere],
        out_specs=(anywhere, vmem, vmem, vmem),
        scratch_shapes=[
            V((seq // STRETCH, STRETCH, HD), bf), V((seq // STRETCH, STRETCH, HD), bf),
            V((4, 512, HD), bf), V((4, 512, HD), bf),
            V((1024, HD), bf), V((HD, 1024), bf),
            V((1024, 512), f32), V((4, 1024, 512), bf), V((1024, 512), bf),
            V((4 * REACH + 1, STRETCH, HD), f32), V((4 * REACH + 1, STRETCH, HD), f32),
            V((seq // STRETCH, STRETCH, HD), bf), V((seq // STRETCH, STRETCH, HD), bf),
            V((nz * 4, STRETCH, HD), bf), V((nz * 4, STRETCH, HD), bf),
            V((2, nz, XROWS, HD), bf), V((2, nz, XROWS, HD), bf),
            V((2, far + 1, XROWS, HD), bf), V((2, far + 1, 2, STRETCH, HD), bf),
            V((2, far + 1, 2, STRETCH, HD), bf), V((2, far + 1, XROWS, HD), bf),
            V((2, far + 1, XROWS, HD), bf), V((2, far + 1, 2, STRETCH, HD), bf),
            V((2, far + 1, 2, STRETCH, HD), bf), V((2, far + 1, XROWS, HD), bf),
            V((2, local, HD), bf), V((2, nh, short, HD), bf),
            V((4, STRETCH, 4 * HD), bf), V((nh, short, 4 * HD), bf), V((nh, short, 4 * HD), bf),
            pltpu.SMEM((4 * REACH,), jnp.int32), pltpu.SMEM((4 * REACH,), f32),
            D((2, AG_N)), D((2, AG_N)), D((2, RS_N)), D((2, RS_N)),
            D((2, nh)), D((2, nh)), D((nh,)), D((nh,)), D((4, 16)), D((4,)),
        ],
        compiler_params=pltpu.CompilerParams(
            collective_id=0, has_side_effects=True, vmem_limit_bytes=56 * 1024 * 1024
        ),
        cost_estimate=pl.CostEstimate(
            flops=3_300_000_000, bytes_accessed=4_000_000, transcendentals=2_100_000
        ),
    )(stretch_order, doc_blocks, query_states, key_states, value_states, out_grad)


def solution(mesh):
    in_specs = (P("ctx", "head"), P("ctx", None), P("ctx", None), P("ctx", "head"), P(), P())
    out_specs = (
        P("ctx", "head"),
        P(("ctx", "head"), None),
        P(("ctx", "head"), None),
        P(("ctx", "head"), None),
    )
    return jax.shard_map(
        on_device, mesh=mesh, in_specs=in_specs, out_specs=out_specs, check_vma=False
    )
```

```python
import functools

import jax
import jax.numpy as jnp
from jax import lax
from jax.experimental import pallas as pl
from jax.experimental.pallas import tpu as pltpu
from jax.sharding import PartitionSpec as P

HD = 128
STRETCH = 128
REACH = 8
MASKED = -1e30
XROWS = 128
LOG2E = 1.4426950408889634

AG_Y, AG_SR, AG_SO, AG_N = 24, 32, 40, 48
RS_S, RS_Y, RS_N = 24, 32, 40
UP, DOWN = 0, 1
ORDER = ((UP, 0), (DOWN, 1), (UP, 1), (DOWN, 2), (UP, 2), (DOWN, 0))


def when(cond, fn):
    if isinstance(cond, bool):
        if cond:
            fn()
    else:
        pl.when(cond)(fn)


def rows(start, size, unit=32):
    return pl.ds(pl.multiple_of(start, unit), size)


def kernel(
    nz, nh,
    order, blocks, q_hbm, k_hbm, v_hbm, g_hbm,
    out_hbm, dq_ref, dk_ref, dv_ref,
    kbuf, vbuf, qcat, gcat, kext, kt, st, wbuf, row_top, contrib_v, contrib_k,
    part_v, part_k, sib_v, sib_k, ysend, yrecv, ring_in, ring_out,
    fin, finrecv, outbuf, dqbuf, dqrecv, slots, bias,
    ag_recv, ag_send, rs_recv, rs_send, fin_recv, fin_send, dq_recv, dq_send, load_sem, out_sem,
):
    ctx = lax.axis_index("ctx")
    head = lax.axis_index("head")
    z, core = ctx // 2, lax.rem(ctx, 2)
    par = lax.rem(head, 2)
    group = head // 2
    local = 4 * STRETCH
    crows = local - 2 * XROWS
    ring_rows = XROWS + crows
    x0, ox0, ring0 = par * 3, 3 - par * 3, par
    far = nz // 2
    short = local // nh
    scale = HD ** (-0.5)

    def zmod(v):
        return lax.rem(v + nz, nz)

    up = {"ctx": zmod(z + 1) * 2 + core}
    down = {"ctx": zmod(z - 1) * 2 + core}
    sib = {"ctx": z * 2 + 1 - core}
    partner = {"head": head + 1 - 2 * par}

    gathered = (kbuf, vbuf)

    def load_kv(t):
        src = (k_hbm, v_hbm)[t].at[:, pl.ds(pl.multiple_of(group * HD, HD), HD)]
        return [
            pltpu.make_async_copy(
                src.at[pl.ds(i * STRETCH, STRETCH)], gathered[t].at[ctx * 4 + i], load_sem.at[t, i]
            )
            for i in range(4)
        ]

    for t in range(2):
        for copy in load_kv(t):
            copy.start()

    def load_qg(n, s, h):
        src, dst_ = ((q_hbm, qcat), (g_hbm, gcat))[n]
        return pltpu.make_async_copy(
            src.at[pl.ds(s * STRETCH, STRETCH), pl.ds(h * HD, HD)],
            dst_.at[s, pl.ds(h * STRETCH, STRETCH)],
            load_sem.at[2 + n, s * 4 + h],
        )

    heads = [(n, s, h) for n in range(2) for s in range(4) for h in range(4)]
    for n, s, h in heads:
        load_qg(n, s, h).start()

    barrier = pltpu.get_barrier_semaphore()
    for who in (up, down, sib):
        pl.semaphore_signal(barrier, inc=1, device_id=who, device_id_type=pl.DeviceIdType.MESH)
    for i in range(1, nh):
        pl.semaphore_signal(
            barrier, inc=1, device_id={"head": lax.rem(head + i, nh)},
            device_id_type=pl.DeviceIdType.MESH,
        )

    zero_row = jnp.zeros((STRETCH, HD), jnp.float32)
    contrib_v[4 * REACH] = zero_row
    contrib_k[4 * REACH] = zero_row
    first_b = XROWS // short
    last_b = (local - XROWS) // short

    def fill(p):
        for t in range(2):
            for i in range(nh // 2):
                finrecv[t, 2 * i + p] = jnp.zeros((short, HD), jnp.bfloat16)

    pl.when(head >= last_b)(lambda: fill(0))
    pl.when(head < first_b)(lambda: fill(1))

    def tables():
        total = order.shape[0]
        for s in range(4):
            own = order[ctx * 4 + s]

            def seek(i, found):
                here = order[i]
                return tuple(
                    jnp.where(here == own - (REACH - 1) + j, i, found[j]) for j in range(REACH)
                )

            found = lax.fori_loop(0, total, seek, (jnp.int32(0),) * REACH)

            def begin(i, carry):
                end, start = carry
                end = end + blocks[i]
                return end, jnp.where(end <= own, end, start)

            _, start = lax.fori_loop(
                0, blocks.shape[0], begin, (jnp.int32(0), jnp.int32(0))
            )
            for j in range(REACH):
                slots[s * REACH + j] = found[j]
                bias[s * REACH + j] = jnp.where(
                    own - (REACH - 1) + j >= start, jnp.float32(0.0), jnp.float32(MASKED)
                )

    tables()
    pl.semaphore_wait(barrier, nh + 2)

    def piece(t, z_of, core_of, start, size):
        return gathered[t].at[pl.ds((z_of * 2 + core_of) * 4 + start, size)]

    def ag_copy(t, z_of, start, size, sem, device):
        ref = piece(t, z_of, core, start, size)
        return pltpu.make_async_remote_copy(
            src_ref=ref, dst_ref=ref, send_sem=ag_send.at[t, sem], recv_sem=ag_recv.at[t, sem],
            device_id=device, device_id_type=pl.DeviceIdType.MESH,
        )

    def ag_wait(t, z_of, core_of, start, size, sem):
        ref = piece(t, z_of, core_of, start, size)
        pltpu.make_async_remote_copy(
            src_ref=ref, dst_ref=ref, send_sem=ag_send.at[t, sem], recv_sem=ag_recv.at[t, sem],
            device_id=up, device_id_type=pl.DeviceIdType.MESH,
        ).wait_recv()

    def at_unit(u):
        return x0 if u == 0 else u

    def chain(way, u):
        return (way * 3 + u) * 4

    def hops(way, u):
        return far if (way == UP) == (u == 0) else far - 1

    def ag_first(t):
        for copy in load_kv(t):
            copy.wait()
        for way, u in ORDER:
            ag_copy(t, z, at_unit(u), 1, chain(way, u), (up, down)[way]).start()
        ag_copy(t, z, ring0, 3, AG_SR, sib).start()
        ag_copy(t, z, ox0, 1, AG_SO, sib).start()

    def ag_partner(t, k):
        zo = zmod(z - k)
        ag_wait(t, zo, core, ox0, 1, AG_Y + k - 1)
        ag_copy(t, zo, ox0, 1, AG_SO + k, sib).start()

        def lower():
            zd = zmod(z + k)
            ag_wait(t, zd, core, ox0, 1, AG_Y + 3 + k)
            ag_copy(t, zd, ox0, 1, AG_SO + nz - k, sib).start()

        when(k < far, lower)

    def ag_step(t, k):
        ag_half(t, k, 0)
        ag_half(t, k, 1)

    def ag_half(t, k, half):
        zo, zd = zmod(z - k), zmod(z + k)
        for way, u in ORDER[3 * half:3 * half + 3]:
            origin, sem, last = (zo, zd)[way], chain(way, u), hops(way, u)

            def pass_on(way=way, u=u, origin=origin, sem=sem, last=last):
                ag_wait(t, origin, core, at_unit(u), 1, sem + k - 1)

                def send():
                    ag_copy(t, origin, at_unit(u), 1, sem + k, (up, down)[way]).start()

                when(k < last, send)
                if u == 0:
                    ag_copy(t, origin, x0, 1, AG_Y + 4 * way + k - 1, partner).start()

            when(k <= last, pass_on)
        if half == 1:
            ag_copy(t, zo, ring0, 3, AG_SR + k, sib).start()
            when(k < far, lambda: ag_copy(t, zd, ring0, 3, AG_SR + nz - k, sib).start())
            when(k > 1, lambda: ag_partner(t, k - 1))

    def ag_finish(t):
        ag_partner(t, far)

        @pl.loop(0, nz)
        def _(d):
            zo = zmod(z - d)
            ag_wait(t, zo, 1 - core, ring0, 3, AG_SR + d)
            ag_wait(t, zo, 1 - core, ox0, 1, AG_SO + d)

    nt = (((1,), (1,)), ((), ()))
    nn = (((1,), (0,)), ((), ()))

    def dot(a, b, dims):
        return lax.dot_general(a, b, dims, preferred_element_type=jnp.float32)

    def fold(value, op):
        return op(value.reshape(STRETCH // 8, 8, value.shape[1]), axis=0)

    def scores(s):
        for j in range(REACH):
            kext[pl.ds(j * STRETCH, STRETCH), :] = kbuf[slots[s * REACH + j]]
        st[...] = dot(kext[...], qcat[s], nt)
        key_at = lax.broadcasted_iota(jnp.int32, (STRETCH, STRETCH), 0)
        query_at = lax.broadcasted_iota(jnp.int32, (STRETCH, STRETCH), 1)
        causal = key_at <= query_at
        diag = pl.ds((REACH - 1) * STRETCH, STRETCH)
        raw = st[diag, :]
        raw = jnp.concatenate(
            [jnp.where(causal, raw[:, h * HD:(h + 1) * HD], MASKED) for h in range(4)], axis=1
        )
        st[diag, :] = raw

        top = fold(raw, jnp.max)
        for j in range(REACH - 1):
            high = fold(st[pl.ds(j * STRETCH, STRETCH), :], jnp.max)
            top = jnp.maximum(top, high + bias[s * REACH + j])
        row_top[...] = jnp.max(top, axis=0, keepdims=True)

    def softmax(s):
        top = row_top[...]
        total = jnp.zeros((8, 512), jnp.float32)
        for j in range(REACH):
            shift = bias[s * REACH + j] - top
            at = pl.ds(j * STRETCH, STRETCH)
            value = jnp.exp2((st[at, :] + shift) * (scale * LOG2E))
            st[at, :] = value
            total = total + fold(value, jnp.sum)
        inverse = 1.0 / jnp.sum(total, axis=0, keepdims=True)
        for j in range(REACH):
            at = pl.ds(j * STRETCH, STRETCH)
            wbuf[s, at, :] = (st[at, :] * inverse).astype(jnp.bfloat16)
        contrib_v[pl.ds(s * REACH, REACH)] = dot(wbuf[s], gcat[s], nn).reshape(REACH, STRETCH, HD)

    per = STRETCH // short

    def key_side(s):
        g = gcat[s]
        for j in range(REACH):
            value = vbuf[slots[s * REACH + j]]
            kext[pl.ds(j * STRETCH, STRETCH), :] = value
            kt[:, pl.ds(j * STRETCH, STRETCH)] = value.T
        st[...] = dot(kext[...], g, nt)
        ot = dot(kt[...], wbuf[s], nn).astype(jnp.bfloat16)
        ot = ot.astype(jnp.float32)
        dots = []
        for h in range(4):
            part = ot[:, h * HD:(h + 1) * HD]
            outbuf[s, :, pl.ds(h * HD, HD)] = part.T.astype(jnp.bfloat16)
            gt = g[h * STRETCH:(h + 1) * STRETCH, :].astype(jnp.float32).T
            dots.append(jnp.sum(gt * part, axis=0, keepdims=True))
        dots = jnp.concatenate(dots, axis=1)
        pltpu.make_async_copy(
            outbuf.at[s],
            out_hbm.at[rows(s * STRETCH, STRETCH, STRETCH)], out_sem.at[s],
        ).start()

        for j in range(REACH):
            at = pl.ds(j * STRETCH, STRETCH)
            w = wbuf[s, at, :].astype(jnp.float32)
            wbuf[s, at, :] = (w * (st[at, :] - dots)).astype(jnp.bfloat16)

        contrib_k[pl.ds(s * REACH, REACH)] = (
            dot(wbuf[s], qcat[s], nn) * scale
        ).reshape(REACH, STRETCH, HD)

    def query_side(s):
        for j in range(REACH):
            kt[:, pl.ds(j * STRETCH, STRETCH)] = kbuf[slots[s * REACH + j]].T
        dqt = dot(kt[...], wbuf[s], nn) * scale
        for h in range(4):
            dqbuf[pl.ds(s * per, per), :, pl.ds(h * HD, HD)] = dqt[
                :, h * HD:(h + 1) * HD
            ].T.reshape(per, short, HD).astype(jnp.bfloat16)

        @pl.loop(0, per)
        def _(i):
            b = s * per + i

            def remote():
                dq_copy(b, head, b).start()

            def own():
                dqrecv[head] = dqbuf[b]

            pl.when(b != head)(remote)
            pl.when(b == head)(own)

    def dq_copy(b, src, to):
        return pltpu.make_async_remote_copy(
            src_ref=dqbuf.at[b], dst_ref=dqrecv.at[src],
            send_sem=dq_send.at[b], recv_sem=dq_recv.at[src],
            device_id={"head": to}, device_id_type=pl.DeviceIdType.MESH,
        )

    contribs = (contrib_k, contrib_v)
    parts = (part_k, part_v)
    sibs = (sib_k, sib_v)

    def build(t, at):
        @pl.loop(0, 4)
        def _(k):
            here = order[at * 4 + k]
            total = None
            for s in range(4):
                delta = order[ctx * 4 + s] - here
                index = jnp.where(
                    (delta >= 0) & (delta < REACH), s * REACH + REACH - 1 - delta, 4 * REACH
                )
                term = contribs[t][index]
                total = term if total is None else total + term
            parts[t][at * 4 + k] = total.astype(jnp.bfloat16)

    def rs_copy(t, src, dst_, sem, device):
        return pltpu.make_async_remote_copy(
            src_ref=src, dst_ref=dst_, send_sem=rs_send.at[t, sem], recv_sem=rs_recv.at[t, sem],
            device_id=device, device_id_type=pl.DeviceIdType.MESH,
        )

    def rs_wait(t, ref, sem):
        rs_copy(t, ref, ref, sem, up).wait_recv()

    def dest(i):
        return zmod(z + far + ((i + 1) // 2) * (2 * lax.rem(i, 2) - 1))

    def rs_build(t):
        @pl.loop(0, nz)
        def _(i):
            rs_dest(t, i)

    def rs_dest(t, i):
        zt = dest(i)
        other = zt * 2 + 1 - core
        build(t, other)
        rs_copy(
            t, parts[t].at[pl.ds(other * 4, 4)], sibs[t].at[pl.ds(i * 4, 4)], RS_S + i, sib
        ).start()
        build(t, zt * 2 + core)

    def place(i):
        if i == nz - 1:
            return z
        delta = far + ((i + 1) // 2) * (2 * (i % 2) - 1)
        return zmod(z + delta)

    def chip_sum(t, i, start, size):
        return (
            parts[t][pl.ds((place(i) * 2 + core) * 4 + start, size)].astype(jnp.float32)
            + sibs[t][pl.ds(i * 4 + start, size)].astype(jnp.float32)
        )

    def own_x(t, i):
        rs_wait(t, yrecv.at[t, i], RS_Y + i)
        return chip_sum(t, i, x0, 1)[0] + yrecv[t, i].astype(jnp.float32)

    def own(t, u, i):
        return own_x(t, i) if u == 0 else chip_sum(t, i, u, 1)[0]

    def rs_chain(t, way, u, k):
        sem, first = chain(way, u), far + 1 - hops(way, u)
        c = way * 3 + u
        i = 2 * (k - 1) if way == UP else max(0, 2 * k - 3)
        if k > first:
            rs_wait(t, ring_in.at[t, c, k - 1], sem + k - 2)
        total = own(t, u, i)
        if k > first:
            total = total + ring_in[t, c, k - 1].astype(jnp.float32)
        ring_out[t, c, k] = total.astype(jnp.bfloat16)
        rs_copy(
            t, ring_out.at[t, c, k], ring_in.at[t, c, k], sem + k - 1, (up, down)[way]
        ).start()

    def rs_begin(t):
        for i in range(nz):
            rs_wait(t, sibs[t].at[pl.ds(i * 4, 4)], RS_S + i)
            ysend[t, i] = chip_sum(t, i, ox0, 1)[0].astype(jnp.bfloat16)
            rs_copy(t, ysend.at[t, i], yrecv.at[t, i], RS_Y + i, partner).start()
            if i == 0:
                rs_chain(t, DOWN, 1, 1)
                rs_chain(t, DOWN, 2, 1)
            if i == 2:
                rs_chain(t, UP, 1, 2)
                rs_chain(t, UP, 2, 2)

    def rs_begin_x(t):
        rs_chain(t, UP, 0, 1)
        rs_chain(t, DOWN, 0, 2)

    def rs_step(t, k):
        for way, u in ORDER:
            if k > far + 1 - hops(way, u):
                rs_chain(t, way, u, k)

    b0 = par * (XROWS // short)
    nb = ring_rows // short
    own_in = (head >= b0) & (head < b0 + nb)

    def fin_copy(t, b, src):
        return pltpu.make_async_remote_copy(
            src_ref=fin.at[t, rows(b * short, short)], dst_ref=finrecv.at[t, src],
            send_sem=fin_send.at[t, b], recv_sem=fin_recv.at[t, src],
            device_id={"head": b}, device_id_type=pl.DeviceIdType.MESH,
        )

    def rs_final(t):
        for u in range(3):
            total = own(t, u, nz - 1)
            for way in (UP, DOWN):
                c = way * 3 + u
                rs_wait(t, ring_in.at[t, c, far], chain(way, u) + far - 1)
                total = total + ring_in[t, c, far].astype(jnp.float32)
            fin[t, rows(at_unit(u) * STRETCH, STRETCH), :] = total.astype(jnp.bfloat16)

        @pl.loop(0, nb)
        def _(i):
            b = b0 + i
            pl.when(b != head)(lambda: fin_copy(t, b, head).start())

            def keep():
                finrecv[t, head] = fin[t, rows(head * short, short), :]

            pl.when(b == head)(keep)

    def rs_out(t, ref):
        @pl.loop(0, nh)
        def _(src):
            p = lax.rem(src, 2)
            sends = ((p == 0) & (head < last_b)) | ((p == 1) & (head >= first_b))
            pl.when(sends & (src != head))(lambda: fin_copy(t, 0, src).wait_recv())

        for g in range(nh // 2):
            ref[:, g * HD:(g + 1) * HD] = (
                finrecv[t, 2 * g].astype(jnp.float32) + finrecv[t, 2 * g + 1].astype(jnp.float32)
            ).astype(jnp.bfloat16)

    ag_first(0)
    ag_first(1)
    ag_step(0, 1)
    ag_step(1, 1)
    ag_step(0, 2)
    ag_step(1, 2)
    ag_step(0, 3)
    ag_step(1, 3)
    ag_step(0, 4)
    ag_finish(0)
    for n, s, h in heads:
        load_qg(n, s, h).wait()

    @pl.loop(0, 4)
    def _(s):
        scores(s)
        pl.when(s < far - 3)(lambda: ag_half(1, s + 4, 0))
        softmax(s)
        pl.when(s < far - 3)(lambda: ag_half(1, s + 4, 1))

    rs_build(1)
    ag_finish(1)
    key_side(0)
    rs_begin(1)
    key_side(1)
    key_side(2)
    key_side(3)
    rs_build(0)
    rs_begin_x(1)
    rs_begin(0)
    rs_step(1, 2)
    query_side(0)
    rs_begin_x(0)
    rs_step(1, 3)
    query_side(1)
    rs_step(0, 2)
    rs_step(1, 4)
    query_side(2)
    rs_step(0, 3)
    rs_final(1)
    query_side(3)
    rs_step(0, 4)
    rs_out(1, dv_ref)
    rs_final(0)
    rs_out(0, dk_ref)

    @pl.loop(0, nh)
    def _(src):
        pl.when(src != head)(lambda: dq_copy(0, src, src).wait_recv())

    for src in range(nh):
        dq_ref[:, src * 4 * HD:(src + 1) * 4 * HD] = dqrecv[src]
    @pl.loop(0, nh)
    def _(b):
        pl.when(b != head)(lambda: dq_copy(b, head, b).wait_send())

    for s in range(4):
        pltpu.make_async_copy(
            outbuf.at[s], out_hbm.at[pl.ds(s * STRETCH, STRETCH)], out_sem.at[s]
        ).wait()
    for t in range(2):
        chains = [(chain(w, u) + far - hops(w, u), hops(w, u)) for w, u in ORDER]
        for first, count, size in [(chain(w, u), hops(w, u), 1) for w, u in ORDER] + [
            (AG_Y, far, 1), (AG_Y + 4, far - 1, 1), (AG_SR, nz, 3), (AG_SO, nz, 1),
        ]:

            @pl.loop(first, first + count)
            def _(sem):
                ag_copy(t, z, 0, size, sem, up).wait_send()

        for first, count, ref in [(f, n, yrecv.at[t, 0]) for f, n in chains] + [
            (RS_S, nz, sibs[t].at[pl.ds(0, 4)]), (RS_Y, nz, yrecv.at[t, 0]),
        ]:

            @pl.loop(first, first + count)
            def _(sem):
                rs_copy(t, ref, ref, sem, up).wait_send()

        @pl.loop(0, nb)
        def _(i):
            pl.when(b0 + i != head)(lambda: fin_copy(t, b0 + i, head).wait_send())


def on_device(query_states, key_states, value_states, out_grad, stretch_order, doc_blocks):
    nz = lax.axis_size("ctx") // 2
    nh = lax.axis_size("head")
    far = nz // 2
    local = 4 * STRETCH
    crows = local - 2 * XROWS
    short = local // nh
    seq = 2 * nz * local
    bf, f32 = jnp.bfloat16, jnp.float32
    anywhere = pl.BlockSpec(memory_space=pl.ANY)
    smem = pl.BlockSpec(memory_space=pltpu.SMEM)
    vmem = pl.BlockSpec(memory_space=pltpu.VMEM)
    V, D = pltpu.VMEM, pltpu.SemaphoreType.DMA
    results = pl.pallas_call(
        functools.partial(kernel, nz, nh),
        out_shape=(
            jax.ShapeDtypeStruct((local, 4 * HD), bf),
            jax.ShapeDtypeStruct((short, nh * 4 * HD), bf),
            jax.ShapeDtypeStruct((short, nh // 2 * HD), bf),
            jax.ShapeDtypeStruct((short, nh // 2 * HD), bf),
        ),
        in_specs=[smem, smem, anywhere, anywhere, anywhere, anywhere],
        out_specs=(anywhere, vmem, vmem, vmem),
        scratch_shapes=[
            V((seq // STRETCH, STRETCH, HD), bf), V((seq // STRETCH, STRETCH, HD), bf),
            V((4, 512, HD), bf), V((4, 512, HD), bf),
            V((1024, HD), bf), V((HD, 1024), bf),
            V((1024, 512), f32), V((4, 1024, 512), bf), V((1, 512), f32),
            V((4 * REACH + 1, STRETCH, HD), f32), V((4 * REACH + 1, STRETCH, HD), f32),
            V((seq // STRETCH, STRETCH, HD), bf), V((seq // STRETCH, STRETCH, HD), bf),
            V((nz * 4, STRETCH, HD), bf), V((nz * 4, STRETCH, HD), bf),
            V((2, nz, XROWS, HD), bf), V((2, nz, XROWS, HD), bf),
            V((2, 6, far + 1, STRETCH, HD), bf), V((2, 6, far + 1, STRETCH, HD), bf),
            V((2, local, HD), bf), V((2, nh, short, HD), bf),
            V((4, STRETCH, 4 * HD), bf), V((nh, short, 4 * HD), bf), V((nh, short, 4 * HD), bf),
            pltpu.SMEM((4 * REACH,), jnp.int32), pltpu.SMEM((4 * REACH,), f32),
            D((2, AG_N)), D((2, AG_N)), D((2, RS_N)), D((2, RS_N)),
            D((2, nh)), D((2, nh)), D((nh,)), D((nh,)), D((4, 16)), D((4,)),
        ],
        compiler_params=pltpu.CompilerParams(
            collective_id=0, has_side_effects=True, vmem_limit_bytes=56 * 1024 * 1024
        ),
        cost_estimate=pl.CostEstimate(
            flops=3_300_000_000, bytes_accessed=4_000_000, transcendentals=2_100_000
        ),
    )(stretch_order, doc_blocks, query_states, key_states, value_states, out_grad)
    return pl.pallas_call(
        settle,
        out_shape=tuple(jax.ShapeDtypeStruct(r.shape, r.dtype) for r in results),
        in_specs=[vmem] * 4,
        out_specs=(vmem,) * 4,
    )(*results)


def settle(*refs):
    for n in range(4):
        refs[4 + n][...] = refs[n][...]


def solution(mesh):
    in_specs = (P("ctx", "head"), P("ctx", None), P("ctx", None), P("ctx", "head"), P(), P())
    out_specs = (
        P("ctx", "head"),
        P(("ctx", "head"), None),
        P(("ctx", "head"), None),
        P(("ctx", "head"), None),
    )
    return jax.shard_map(
        on_device, mesh=mesh, in_specs=in_specs, out_specs=out_specs, check_vma=False
    )
```

```python
import functools

import jax
import jax.numpy as jnp
from jax import lax
from jax.experimental import pallas as pl
from jax.experimental.pallas import tpu as pltpu
from jax.sharding import PartitionSpec as P

HD = 128
STRETCH = 128
REACH = 8
MASKED = -1e30
XROWS = 128
LOG2E = 1.4426950408889634

AG_Y, AG_SR, AG_SO, AG_N = 24, 32, 40, 48
RS_S, RS_Y, RS_N = 24, 32, 40
UP, DOWN = 0, 1
ORDER = ((UP, 0), (DOWN, 1), (UP, 1), (DOWN, 2), (UP, 2), (DOWN, 0))


def when(cond, fn):
    if isinstance(cond, bool):
        if cond:
            fn()
    else:
        pl.when(cond)(fn)


def rows(start, size, unit=32):
    return pl.ds(pl.multiple_of(start, unit), size)


def kernel(
    nz, nh,
    order, blocks, q_hbm, k_hbm, v_hbm, g_hbm,
    out_hbm, dq_ref, dk_ref, dv_ref,
    kbuf, vbuf, qcat, gcat, kext, kt, st, wbuf, row_top, contrib_v, contrib_k,
    part_v, part_k, sib_v, sib_k, ysend, yrecv, ring_in, ring_out,
    fin, finrecv, outbuf, dqbuf, dqrecv, slots, bias,
    ag_recv, ag_send, rs_recv, rs_send, fin_recv, fin_send, dq_recv, dq_send, load_sem, out_sem,
):
    ctx = lax.axis_index("ctx")
    head = lax.axis_index("head")
    z, core = ctx // 2, lax.rem(ctx, 2)
    par = lax.rem(head, 2)
    group = head // 2
    local = 4 * STRETCH
    crows = local - 2 * XROWS
    ring_rows = XROWS + crows
    x0, ox0, ring0 = par * 3, 3 - par * 3, par
    far = nz // 2
    short = local // nh
    scale = HD ** (-0.5)

    def zmod(v):
        return lax.rem(v + nz, nz)

    up = {"ctx": zmod(z + 1) * 2 + core}
    down = {"ctx": zmod(z - 1) * 2 + core}
    sib = {"ctx": z * 2 + 1 - core}
    partner = {"head": head + 1 - 2 * par}

    gathered = (kbuf, vbuf)

    def load_kv(t):
        src = (k_hbm, v_hbm)[t].at[:, pl.ds(pl.multiple_of(group * HD, HD), HD)]
        return [
            pltpu.make_async_copy(
                src.at[pl.ds(i * STRETCH, STRETCH)], gathered[t].at[ctx * 4 + i], load_sem.at[t, i]
            )
            for i in range(4)
        ]

    for t in range(2):
        for copy in load_kv(t):
            copy.start()

    def load_qg(n, s, h):
        src, dst_ = ((q_hbm, qcat), (g_hbm, gcat))[n]
        return pltpu.make_async_copy(
            src.at[pl.ds(s * STRETCH, STRETCH), pl.ds(h * HD, HD)],
            dst_.at[s, pl.ds(h * STRETCH, STRETCH)],
            load_sem.at[2 + n, s * 4 + h],
        )

    heads = [(n, s, h) for n in range(2) for s in range(4) for h in range(4)]
    for n, s, h in heads:
        load_qg(n, s, h).start()

    barrier = pltpu.get_barrier_semaphore()
    for who in (up, down, sib):
        pl.semaphore_signal(barrier, inc=1, device_id=who, device_id_type=pl.DeviceIdType.MESH)
    for i in range(1, nh):
        pl.semaphore_signal(
            barrier, inc=1, device_id={"head": lax.rem(head + i, nh)},
            device_id_type=pl.DeviceIdType.MESH,
        )

    zero_row = jnp.zeros((STRETCH, HD), jnp.float32)
    contrib_v[4 * REACH] = zero_row
    contrib_k[4 * REACH] = zero_row
    first_b = XROWS // short
    last_b = (local - XROWS) // short

    def fill(p):
        for t in range(2):
            for i in range(nh // 2):
                finrecv[t, 2 * i + p] = jnp.zeros((short, HD), jnp.bfloat16)

    pl.when(head >= last_b)(lambda: fill(0))
    pl.when(head < first_b)(lambda: fill(1))

    def tables():
        total = order.shape[0]
        for s in range(4):
            own = order[ctx * 4 + s]

            def seek(i, found):
                here = order[i]
                return tuple(
                    jnp.where(here == own - (REACH - 1) + j, i, found[j]) for j in range(REACH)
                )

            found = lax.fori_loop(0, total, seek, (jnp.int32(0),) * REACH)

            def begin(i, carry):
                end, start = carry
                end = end + blocks[i]
                return end, jnp.where(end <= own, end, start)

            _, start = lax.fori_loop(
                0, blocks.shape[0], begin, (jnp.int32(0), jnp.int32(0))
            )
            for j in range(REACH):
                slots[s * REACH + j] = found[j]
                bias[s * REACH + j] = jnp.where(
                    own - (REACH - 1) + j >= start, jnp.float32(0.0), jnp.float32(MASKED)
                )

    tables()
    pl.semaphore_wait(barrier, nh + 2)

    def piece(t, z_of, core_of, start, size):
        return gathered[t].at[pl.ds((z_of * 2 + core_of) * 4 + start, size)]

    def ag_copy(t, z_of, start, size, sem, device):
        ref = piece(t, z_of, core, start, size)
        return pltpu.make_async_remote_copy(
            src_ref=ref, dst_ref=ref, send_sem=ag_send.at[t, sem], recv_sem=ag_recv.at[t, sem],
            device_id=device, device_id_type=pl.DeviceIdType.MESH,
        )

    def ag_wait(t, z_of, core_of, start, size, sem):
        ref = piece(t, z_of, core_of, start, size)
        pltpu.make_async_remote_copy(
            src_ref=ref, dst_ref=ref, send_sem=ag_send.at[t, sem], recv_sem=ag_recv.at[t, sem],
            device_id=up, device_id_type=pl.DeviceIdType.MESH,
        ).wait_recv()

    def at_unit(u):
        return x0 if u == 0 else u

    def chain(way, u):
        return (way * 3 + u) * 4

    def hops(way, u):
        return far if (way == UP) == (u == 0) else far - 1

    def ag_first(t):
        for copy in load_kv(t):
            copy.wait()
        for way, u in ORDER:
            ag_copy(t, z, at_unit(u), 1, chain(way, u), (up, down)[way]).start()
        ag_copy(t, z, ring0, 3, AG_SR, sib).start()
        ag_copy(t, z, ox0, 1, AG_SO, sib).start()

    def ag_partner(t, k):
        zo = zmod(z - k)
        ag_wait(t, zo, core, ox0, 1, AG_Y + k - 1)
        ag_copy(t, zo, ox0, 1, AG_SO + k, sib).start()

        def lower():
            zd = zmod(z + k)
            ag_wait(t, zd, core, ox0, 1, AG_Y + 3 + k)
            ag_copy(t, zd, ox0, 1, AG_SO + nz - k, sib).start()

        when(k < far, lower)

    def ag_step(t, k):
        ag_half(t, k, 0)
        ag_half(t, k, 1)

    def ag_half(t, k, half):
        zo, zd = zmod(z - k), zmod(z + k)
        for way, u in ORDER[3 * half:3 * half + 3]:
            origin, sem, last = (zo, zd)[way], chain(way, u), hops(way, u)

            def pass_on(way=way, u=u, origin=origin, sem=sem, last=last):
                ag_wait(t, origin, core, at_unit(u), 1, sem + k - 1)

                def send():
                    ag_copy(t, origin, at_unit(u), 1, sem + k, (up, down)[way]).start()

                when(k < last, send)
                if u == 0:
                    ag_copy(t, origin, x0, 1, AG_Y + 4 * way + k - 1, partner).start()

            when(k <= last, pass_on)
        if half == 1:
            ag_copy(t, zo, ring0, 3, AG_SR + k, sib).start()
            when(k < far, lambda: ag_copy(t, zd, ring0, 3, AG_SR + nz - k, sib).start())
            when(k > 1, lambda: ag_partner(t, k - 1))

    def ag_finish(t):
        ag_partner(t, far)

        @pl.loop(0, nz)
        def _(d):
            zo = zmod(z - d)
            ag_wait(t, zo, 1 - core, ring0, 3, AG_SR + d)
            ag_wait(t, zo, 1 - core, ox0, 1, AG_SO + d)

    nt = (((1,), (1,)), ((), ()))
    nn = (((1,), (0,)), ((), ()))

    def dot(a, b, dims):
        return lax.dot_general(a, b, dims, preferred_element_type=jnp.float32)

    def fold(value, op):
        return op(value.reshape(STRETCH // 8, 8, value.shape[1]), axis=0)

    def scores(s):
        for j in range(REACH):
            kext[pl.ds(j * STRETCH, STRETCH), :] = kbuf[slots[s * REACH + j]]
        st[...] = dot(kext[...], qcat[s], nt)
        key_at = lax.broadcasted_iota(jnp.int32, (STRETCH, STRETCH), 0)
        query_at = lax.broadcasted_iota(jnp.int32, (STRETCH, STRETCH), 1)
        causal = key_at <= query_at
        diag = pl.ds((REACH - 1) * STRETCH, STRETCH)
        raw = st[diag, :]
        raw = jnp.concatenate(
            [jnp.where(causal, raw[:, h * HD:(h + 1) * HD], MASKED) for h in range(4)], axis=1
        )
        st[diag, :] = raw

        top = fold(raw, jnp.max)
        for j in range(REACH - 1):
            high = fold(st[pl.ds(j * STRETCH, STRETCH), :], jnp.max)
            top = jnp.maximum(top, high + bias[s * REACH + j])
        row_top[...] = jnp.max(top, axis=0, keepdims=True)

    def softmax(s):
        top = row_top[...]
        total = jnp.zeros((8, 512), jnp.float32)
        for j in range(REACH):
            shift = bias[s * REACH + j] - top
            at = pl.ds(j * STRETCH, STRETCH)
            value = jnp.exp2((st[at, :] + shift) * (scale * LOG2E))
            st[at, :] = value
            total = total + fold(value, jnp.sum)
        inverse = 1.0 / jnp.sum(total, axis=0, keepdims=True)
        for j in range(REACH):
            at = pl.ds(j * STRETCH, STRETCH)
            wbuf[s, at, :] = (st[at, :] * inverse).astype(jnp.bfloat16)
        contrib_v[pl.ds(s * REACH, REACH)] = dot(wbuf[s], gcat[s], nn).reshape(REACH, STRETCH, HD)

    per = STRETCH // short

    def key_side(s):
        g = gcat[s]
        for j in range(REACH):
            value = vbuf[slots[s * REACH + j]]
            kext[pl.ds(j * STRETCH, STRETCH), :] = value
            kt[:, pl.ds(j * STRETCH, STRETCH)] = value.T
        st[...] = dot(kext[...], g, nt)
        ot = dot(kt[...], wbuf[s], nn).astype(jnp.bfloat16)
        ot = ot.astype(jnp.float32)
        dots = []
        for h in range(4):
            part = ot[:, h * HD:(h + 1) * HD]
            outbuf[s, :, pl.ds(h * HD, HD)] = part.T.astype(jnp.bfloat16)
            gt = g[h * STRETCH:(h + 1) * STRETCH, :].astype(jnp.float32).T
            dots.append(jnp.sum(gt * part, axis=0, keepdims=True))
        dots = jnp.concatenate(dots, axis=1)
        pltpu.make_async_copy(
            outbuf.at[s],
            out_hbm.at[rows(s * STRETCH, STRETCH, STRETCH)], out_sem.at[s],
        ).start()

        for j in range(REACH):
            at = pl.ds(j * STRETCH, STRETCH)
            w = wbuf[s, at, :].astype(jnp.float32)
            wbuf[s, at, :] = (w * (st[at, :] - dots)).astype(jnp.bfloat16)

        contrib_k[pl.ds(s * REACH, REACH)] = (
            dot(wbuf[s], qcat[s], nn) * scale
        ).reshape(REACH, STRETCH, HD)

    def query_side(s):
        for j in range(REACH):
            kt[:, pl.ds(j * STRETCH, STRETCH)] = kbuf[slots[s * REACH + j]].T
        dqt = dot(kt[...], wbuf[s], nn) * scale
        for h in range(4):
            dqbuf[pl.ds(s * per, per), :, pl.ds(h * HD, HD)] = dqt[
                :, h * HD:(h + 1) * HD
            ].T.reshape(per, short, HD).astype(jnp.bfloat16)

        @pl.loop(0, per)
        def _(i):
            b = s * per + i

            def remote():
                dq_copy(b, head, b).start()

            def own():
                dqrecv[head] = dqbuf[b]

            pl.when(b != head)(remote)
            pl.when(b == head)(own)

    def dq_copy(b, src, to):
        return pltpu.make_async_remote_copy(
            src_ref=dqbuf.at[b], dst_ref=dqrecv.at[src],
            send_sem=dq_send.at[b], recv_sem=dq_recv.at[src],
            device_id={"head": to}, device_id_type=pl.DeviceIdType.MESH,
        )

    contribs = (contrib_k, contrib_v)
    parts = (part_k, part_v)
    sibs = (sib_k, sib_v)

    def build(t, at):
        @pl.loop(0, 4)
        def _(k):
            here = order[at * 4 + k]
            total = None
            for s in range(4):
                delta = order[ctx * 4 + s] - here
                index = jnp.where(
                    (delta >= 0) & (delta < REACH), s * REACH + REACH - 1 - delta, 4 * REACH
                )
                term = contribs[t][index]
                total = term if total is None else total + term
            parts[t][at * 4 + k] = total.astype(jnp.bfloat16)

    def rs_copy(t, src, dst_, sem, device):
        return pltpu.make_async_remote_copy(
            src_ref=src, dst_ref=dst_, send_sem=rs_send.at[t, sem], recv_sem=rs_recv.at[t, sem],
            device_id=device, device_id_type=pl.DeviceIdType.MESH,
        )

    def rs_wait(t, ref, sem):
        rs_copy(t, ref, ref, sem, up).wait_recv()

    def dest(i):
        return zmod(z + far + ((i + 1) // 2) * (2 * lax.rem(i, 2) - 1))

    def rs_build(t):
        @pl.loop(0, nz)
        def _(i):
            rs_dest(t, i)

    def rs_dest(t, i):
        zt = dest(i)
        other = zt * 2 + 1 - core
        build(t, other)
        rs_copy(
            t, parts[t].at[pl.ds(other * 4, 4)], sibs[t].at[pl.ds(i * 4, 4)], RS_S + i, sib
        ).start()
        build(t, zt * 2 + core)

    def place(i):
        if i == nz - 1:
            return z
        delta = far + ((i + 1) // 2) * (2 * (i % 2) - 1)
        return zmod(z + delta)

    def chip_sum(t, i, start, size):
        return (
            parts[t][pl.ds((place(i) * 2 + core) * 4 + start, size)].astype(jnp.float32)
            + sibs[t][pl.ds(i * 4 + start, size)].astype(jnp.float32)
        )

    def own_x(t, i):
        rs_wait(t, yrecv.at[t, i], RS_Y + i)
        return chip_sum(t, i, x0, 1)[0] + yrecv[t, i].astype(jnp.float32)

    def own(t, u, i):
        return own_x(t, i) if u == 0 else chip_sum(t, i, u, 1)[0]

    def rs_chain(t, way, u, k):
        sem, first = chain(way, u), far + 1 - hops(way, u)
        c = way * 3 + u
        i = 2 * (k - 1) if way == UP else max(0, 2 * k - 3)
        if k > first:
            rs_wait(t, ring_in.at[t, c, k - 1], sem + k - 2)
        total = own(t, u, i)
        if k > first:
            total = total + ring_in[t, c, k - 1].astype(jnp.float32)
        ring_out[t, c, k] = total.astype(jnp.bfloat16)
        rs_copy(
            t, ring_out.at[t, c, k], ring_in.at[t, c, k], sem + k - 1, (up, down)[way]
        ).start()

    def rs_begin(t):
        for i in range(nz):
            rs_wait(t, sibs[t].at[pl.ds(i * 4, 4)], RS_S + i)
            ysend[t, i] = chip_sum(t, i, ox0, 1)[0].astype(jnp.bfloat16)
            rs_copy(t, ysend.at[t, i], yrecv.at[t, i], RS_Y + i, partner).start()
            if i == 0:
                rs_chain(t, DOWN, 1, 1)
                rs_chain(t, DOWN, 2, 1)
            if i == 2:
                rs_chain(t, UP, 1, 2)
                rs_chain(t, UP, 2, 2)

    def rs_begin_x(t):
        rs_chain(t, UP, 0, 1)
        rs_chain(t, DOWN, 0, 2)

    def rs_step(t, k):
        for way, u in ORDER:
            if k > far + 1 - hops(way, u):
                rs_chain(t, way, u, k)

    b0 = par * (XROWS // short)
    nb = ring_rows // short
    own_in = (head >= b0) & (head < b0 + nb)

    def fin_copy(t, b, src):
        return pltpu.make_async_remote_copy(
            src_ref=fin.at[t, rows(b * short, short)], dst_ref=finrecv.at[t, src],
            send_sem=fin_send.at[t, b], recv_sem=fin_recv.at[t, src],
            device_id={"head": b}, device_id_type=pl.DeviceIdType.MESH,
        )

    def rs_final(t):
        for u in range(3):
            total = own(t, u, nz - 1)
            for way in (UP, DOWN):
                c = way * 3 + u
                rs_wait(t, ring_in.at[t, c, far], chain(way, u) + far - 1)
                total = total + ring_in[t, c, far].astype(jnp.float32)
            fin[t, rows(at_unit(u) * STRETCH, STRETCH), :] = total.astype(jnp.bfloat16)

        @pl.loop(0, nb)
        def _(i):
            b = b0 + i
            pl.when(b != head)(lambda: fin_copy(t, b, head).start())

            def keep():
                finrecv[t, head] = fin[t, rows(head * short, short), :]

            pl.when(b == head)(keep)

    def rs_out(t, ref):
        @pl.loop(0, nh)
        def _(src):
            p = lax.rem(src, 2)
            sends = ((p == 0) & (head < last_b)) | ((p == 1) & (head >= first_b))
            pl.when(sends & (src != head))(lambda: fin_copy(t, 0, src).wait_recv())

        for g in range(nh // 2):
            ref[:, g * HD:(g + 1) * HD] = (
                finrecv[t, 2 * g].astype(jnp.float32) + finrecv[t, 2 * g + 1].astype(jnp.float32)
            ).astype(jnp.bfloat16)

    ag_first(0)
    ag_first(1)
    ag_step(0, 1)
    ag_step(1, 1)
    ag_step(0, 2)
    ag_step(1, 2)
    ag_step(0, 3)
    ag_step(1, 3)
    ag_step(0, 4)
    ag_finish(0)
    for n, s, h in heads:
        load_qg(n, s, h).wait()

    @pl.loop(0, 4)
    def _(s):
        scores(s)
        pl.when(s < far - 3)(lambda: ag_half(1, s + 4, 0))
        softmax(s)
        pl.when(s < far - 3)(lambda: ag_half(1, s + 4, 1))

    rs_build(1)
    ag_finish(1)
    key_side(0)
    rs_begin(1)
    key_side(1)
    key_side(2)
    key_side(3)
    rs_build(0)
    rs_begin_x(1)
    rs_begin(0)
    rs_step(1, 2)
    query_side(0)
    rs_begin_x(0)
    rs_step(1, 3)
    query_side(1)
    rs_step(0, 2)
    rs_step(1, 4)
    query_side(2)
    rs_step(0, 3)
    rs_final(1)
    query_side(3)
    rs_step(0, 4)
    rs_out(1, dv_ref)
    rs_final(0)

    @pl.loop(0, nh)
    def _(src):
        pl.when(src != head)(lambda: dq_copy(0, src, src).wait_recv())

    for src in range(nh):
        dq_ref[:, src * 4 * HD:(src + 1) * 4 * HD] = dqrecv[src]
    @pl.loop(0, nh)
    def _(b):
        pl.when(b != head)(lambda: dq_copy(b, head, b).wait_send())

    for s in range(4):
        pltpu.make_async_copy(
            outbuf.at[s], out_hbm.at[pl.ds(s * STRETCH, STRETCH)], out_sem.at[s]
        ).wait()
    for t in range(2):
        chains = [(chain(w, u) + far - hops(w, u), hops(w, u)) for w, u in ORDER]
        for first, count, size in [(chain(w, u), hops(w, u), 1) for w, u in ORDER] + [
            (AG_Y, far, 1), (AG_Y + 4, far - 1, 1), (AG_SR, nz, 3), (AG_SO, nz, 1),
        ]:

            @pl.loop(first, first + count)
            def _(sem):
                ag_copy(t, z, 0, size, sem, up).wait_send()

        for first, count, ref in [(f, n, yrecv.at[t, 0]) for f, n in chains] + [
            (RS_S, nz, sibs[t].at[pl.ds(0, 4)]), (RS_Y, nz, yrecv.at[t, 0]),
        ]:

            @pl.loop(first, first + count)
            def _(sem):
                rs_copy(t, ref, ref, sem, up).wait_send()

        @pl.loop(0, nb)
        def _(i):
            pl.when(b0 + i != head)(lambda: fin_copy(t, b0 + i, head).wait_send())

    rs_out(0, dk_ref)


def on_device(query_states, key_states, value_states, out_grad, stretch_order, doc_blocks):
    nz = lax.axis_size("ctx") // 2
    nh = lax.axis_size("head")
    far = nz // 2
    local = 4 * STRETCH
    crows = local - 2 * XROWS
    short = local // nh
    seq = 2 * nz * local
    bf, f32 = jnp.bfloat16, jnp.float32
    anywhere = pl.BlockSpec(memory_space=pl.ANY)
    smem = pl.BlockSpec(memory_space=pltpu.SMEM)
    vmem = pl.BlockSpec(memory_space=pltpu.VMEM)
    V, D = pltpu.VMEM, pltpu.SemaphoreType.DMA
    results = pl.pallas_call(
        functools.partial(kernel, nz, nh),
        out_shape=(
            jax.ShapeDtypeStruct((local, 4 * HD), bf),
            jax.ShapeDtypeStruct((short, nh * 4 * HD), bf),
            jax.ShapeDtypeStruct((short, nh // 2 * HD), bf),
            jax.ShapeDtypeStruct((short, nh // 2 * HD), bf),
        ),
        in_specs=[smem, smem, anywhere, anywhere, anywhere, anywhere],
        out_specs=(anywhere, vmem, vmem, vmem),
        scratch_shapes=[
            V((seq // STRETCH, STRETCH, HD), bf), V((seq // STRETCH, STRETCH, HD), bf),
            V((4, 512, HD), bf), V((4, 512, HD), bf),
            V((1024, HD), bf), V((HD, 1024), bf),
            V((1024, 512), f32), V((4, 1024, 512), bf), V((1, 512), f32),
            V((4 * REACH + 1, STRETCH, HD), f32), V((4 * REACH + 1, STRETCH, HD), f32),
            V((seq // STRETCH, STRETCH, HD), bf), V((seq // STRETCH, STRETCH, HD), bf),
            V((nz * 4, STRETCH, HD), bf), V((nz * 4, STRETCH, HD), bf),
            V((2, nz, XROWS, HD), bf), V((2, nz, XROWS, HD), bf),
            V((2, 6, far + 1, STRETCH, HD), bf), V((2, 6, far + 1, STRETCH, HD), bf),
            V((2, local, HD), bf), V((2, nh, short, HD), bf),
            V((4, STRETCH, 4 * HD), bf), V((nh, short, 4 * HD), bf), V((nh, short, 4 * HD), bf),
            pltpu.SMEM((4 * REACH,), jnp.int32), pltpu.SMEM((4 * REACH,), f32),
            D((2, AG_N)), D((2, AG_N)), D((2, RS_N)), D((2, RS_N)),
            D((2, nh)), D((2, nh)), D((nh,)), D((nh,)), D((4, 16)), D((4,)),
        ],
        compiler_params=pltpu.CompilerParams(
            collective_id=0, has_side_effects=True, vmem_limit_bytes=56 * 1024 * 1024
        ),
        cost_estimate=pl.CostEstimate(
            flops=3_300_000_000, bytes_accessed=4_000_000, transcendentals=2_100_000
        ),
    )(stretch_order, doc_blocks, query_states, key_states, value_states, out_grad)
    return pl.pallas_call(
        settle,
        out_shape=tuple(jax.ShapeDtypeStruct(r.shape, r.dtype) for r in results),
        in_specs=[vmem] * 4,
        out_specs=(vmem,) * 4,
    )(*results)


def settle(*refs):
    for n in range(4):
        refs[4 + n][...] = refs[n][...]


def solution(mesh):
    in_specs = (P("ctx", "head"), P("ctx", None), P("ctx", None), P("ctx", "head"), P(), P())
    out_specs = (
        P("ctx", "head"),
        P(("ctx", "head"), None),
        P(("ctx", "head"), None),
        P(("ctx", "head"), None),
    )
    return jax.shard_map(
        on_device, mesh=mesh, in_specs=in_specs, out_specs=out_specs, check_vma=False
    )
```

```python
import functools

import jax
import jax.numpy as jnp
from jax import lax
from jax.experimental import pallas as pl
from jax.experimental.pallas import tpu as pltpu
from jax.sharding import PartitionSpec as P

HD = 128
STRETCH = 128
REACH = 8
MASKED = -1e30
XROWS = 128
LOG2E = 1.4426950408889634

AG_Y, AG_SR, AG_SO, AG_N = 24, 32, 40, 48
RS_S, RS_Y, RS_N = 24, 32, 40
UP, DOWN = 0, 1
ORDER = ((UP, 0), (DOWN, 0), (DOWN, 1), (UP, 1), (DOWN, 2), (UP, 2))


def when(cond, fn):
    if isinstance(cond, bool):
        if cond:
            fn()
    else:
        pl.when(cond)(fn)


def rows(start, size, unit=32):
    return pl.ds(pl.multiple_of(start, unit), size)


def kernel(
    nz, nh,
    order, blocks, q_hbm, k_hbm, v_hbm, g_hbm,
    out_hbm, dq_ref, dk_ref, dv_ref,
    kbuf, vbuf, qcat, gcat, kext, kt, st, wbuf, row_top, contrib_v, contrib_k,
    part_v, part_k, sib_v, sib_k, ysend, yrecv, ring_in, ring_out,
    fin, finrecv, outbuf, dqbuf, dqrecv, slots, bias,
    ag_recv, ag_send, rs_recv, rs_send, fin_recv, fin_send, dq_recv, dq_send, load_sem, out_sem,
):
    ctx = lax.axis_index("ctx")
    head = lax.axis_index("head")
    z, core = ctx // 2, lax.rem(ctx, 2)
    par = lax.rem(head, 2)
    group = head // 2
    local = 4 * STRETCH
    crows = local - 2 * XROWS
    ring_rows = XROWS + crows
    x0, ox0, ring0 = par * 3, 3 - par * 3, par
    far = nz // 2
    short = local // nh
    scale = HD ** (-0.5)

    def zmod(v):
        return lax.rem(v + nz, nz)

    up = {"ctx": zmod(z + 1) * 2 + core}
    down = {"ctx": zmod(z - 1) * 2 + core}
    sib = {"ctx": z * 2 + 1 - core}
    partner = {"head": head + 1 - 2 * par}

    gathered = (kbuf, vbuf)

    def load_kv(t):
        src = (k_hbm, v_hbm)[t].at[:, pl.ds(pl.multiple_of(group * HD, HD), HD)]
        return [
            pltpu.make_async_copy(
                src.at[pl.ds(i * STRETCH, STRETCH)], gathered[t].at[ctx * 4 + i], load_sem.at[t, i]
            )
            for i in range(4)
        ]

    for t in range(2):
        for copy in load_kv(t):
            copy.start()

    def load_qg(n, s, h):
        src, dst_ = ((q_hbm, qcat), (g_hbm, gcat))[n]
        return pltpu.make_async_copy(
            src.at[pl.ds(s * STRETCH, STRETCH), pl.ds(h * HD, HD)],
            dst_.at[s, pl.ds(h * STRETCH, STRETCH)],
            load_sem.at[2 + n, s * 4 + h],
        )

    heads = [(n, s, h) for n in range(2) for s in range(4) for h in range(4)]
    for n, s, h in heads:
        load_qg(n, s, h).start()

    barrier = pltpu.get_barrier_semaphore()
    for who in (up, down, sib):
        pl.semaphore_signal(barrier, inc=1, device_id=who, device_id_type=pl.DeviceIdType.MESH)
    for i in range(1, nh):
        pl.semaphore_signal(
            barrier, inc=1, device_id={"head": lax.rem(head + i, nh)},
            device_id_type=pl.DeviceIdType.MESH,
        )

    zero_row = jnp.zeros((STRETCH, HD), jnp.float32)
    contrib_v[4 * REACH] = zero_row
    contrib_k[4 * REACH] = zero_row
    first_b = XROWS // short
    last_b = (local - XROWS) // short

    def fill(p):
        for t in range(2):
            for i in range(nh // 2):
                finrecv[t, 2 * i + p] = jnp.zeros((short, HD), jnp.bfloat16)

    pl.when(head >= last_b)(lambda: fill(0))
    pl.when(head < first_b)(lambda: fill(1))

    def tables():
        total = order.shape[0]
        for s in range(4):
            own = order[ctx * 4 + s]

            def seek(i, found):
                here = order[i]
                return tuple(
                    jnp.where(here == own - (REACH - 1) + j, i, found[j]) for j in range(REACH)
                )

            found = lax.fori_loop(0, total, seek, (jnp.int32(0),) * REACH)

            def begin(i, carry):
                end, start = carry
                end = end + blocks[i]
                return end, jnp.where(end <= own, end, start)

            _, start = lax.fori_loop(
                0, blocks.shape[0], begin, (jnp.int32(0), jnp.int32(0))
            )
            for j in range(REACH):
                slots[s * REACH + j] = found[j]
                bias[s * REACH + j] = jnp.where(
                    own - (REACH - 1) + j >= start, jnp.float32(0.0), jnp.float32(MASKED)
                )

    tables()
    pl.semaphore_wait(barrier, nh + 2)

    def piece(t, z_of, core_of, start, size):
        return gathered[t].at[pl.ds((z_of * 2 + core_of) * 4 + start, size)]

    def ag_copy(t, z_of, start, size, sem, device):
        ref = piece(t, z_of, core, start, size)
        return pltpu.make_async_remote_copy(
            src_ref=ref, dst_ref=ref, send_sem=ag_send.at[t, sem], recv_sem=ag_recv.at[t, sem],
            device_id=device, device_id_type=pl.DeviceIdType.MESH,
        )

    def ag_wait(t, z_of, core_of, start, size, sem):
        ref = piece(t, z_of, core_of, start, size)
        pltpu.make_async_remote_copy(
            src_ref=ref, dst_ref=ref, send_sem=ag_send.at[t, sem], recv_sem=ag_recv.at[t, sem],
            device_id=up, device_id_type=pl.DeviceIdType.MESH,
        ).wait_recv()

    def at_unit(u):
        return x0 if u == 0 else u

    def chain(way, u):
        return (way * 3 + u) * 4

    def hops(way, u):
        return far if (way == UP) == (u == 0) else far - 1

    def ag_first(t):
        for copy in load_kv(t):
            copy.wait()
        for way, u in ORDER:
            ag_copy(t, z, at_unit(u), 1, chain(way, u), (up, down)[way]).start()
        ag_copy(t, z, ring0, 3, AG_SR, sib).start()
        ag_copy(t, z, ox0, 1, AG_SO, sib).start()

    def ag_partner(t, k):
        zo = zmod(z - k)
        ag_wait(t, zo, core, ox0, 1, AG_Y + k - 1)
        ag_copy(t, zo, ox0, 1, AG_SO + k, sib).start()

        def lower():
            zd = zmod(z + k)
            ag_wait(t, zd, core, ox0, 1, AG_Y + 3 + k)
            ag_copy(t, zd, ox0, 1, AG_SO + nz - k, sib).start()

        when(k < far, lower)

    def ag_step(t, k):
        ag_half(t, k, 0)
        ag_half(t, k, 1)

    def ag_half(t, k, half):
        zo, zd = zmod(z - k), zmod(z + k)
        for way, u in ORDER[3 * half:3 * half + 3]:
            origin, sem, last = (zo, zd)[way], chain(way, u), hops(way, u)

            def pass_on(way=way, u=u, origin=origin, sem=sem, last=last):
                ag_wait(t, origin, core, at_unit(u), 1, sem + k - 1)

                def send():
                    ag_copy(t, origin, at_unit(u), 1, sem + k, (up, down)[way]).start()

                when(k < last, send)
                if u == 0:
                    ag_copy(t, origin, x0, 1, AG_Y + 4 * way + k - 1, partner).start()

            when(k <= last, pass_on)
        if half == 1:
            ag_copy(t, zo, ring0, 3, AG_SR + k, sib).start()
            when(k < far, lambda: ag_copy(t, zd, ring0, 3, AG_SR + nz - k, sib).start())
            when(k > 1, lambda: ag_partner(t, k - 1))

    def ag_finish(t):
        ag_partner(t, far)

        @pl.loop(0, nz)
        def _(d):
            zo = zmod(z - d)
            ag_wait(t, zo, 1 - core, ring0, 3, AG_SR + d)
            ag_wait(t, zo, 1 - core, ox0, 1, AG_SO + d)

    nt = (((1,), (1,)), ((), ()))
    nn = (((1,), (0,)), ((), ()))

    def dot(a, b, dims):
        return lax.dot_general(a, b, dims, preferred_element_type=jnp.float32)

    def fold(value, op):
        return op(value.reshape(STRETCH // 8, 8, value.shape[1]), axis=0)

    def scores(s):
        for j in range(REACH):
            kext[pl.ds(j * STRETCH, STRETCH), :] = kbuf[slots[s * REACH + j]]
        st[...] = dot(kext[...], qcat[s], nt)
        key_at = lax.broadcasted_iota(jnp.int32, (STRETCH, STRETCH), 0)
        query_at = lax.broadcasted_iota(jnp.int32, (STRETCH, STRETCH), 1)
        causal = key_at <= query_at
        diag = pl.ds((REACH - 1) * STRETCH, STRETCH)
        raw = st[diag, :]
        raw = jnp.concatenate(
            [jnp.where(causal, raw[:, h * HD:(h + 1) * HD], MASKED) for h in range(4)], axis=1
        )
        st[diag, :] = raw

        top = fold(raw, jnp.max)
        for j in range(REACH - 1):
            high = fold(st[pl.ds(j * STRETCH, STRETCH), :], jnp.max)
            top = jnp.maximum(top, high + bias[s * REACH + j])
        row_top[...] = jnp.max(top, axis=0, keepdims=True)

    def softmax(s):
        top = row_top[...]
        total = jnp.zeros((8, 512), jnp.float32)
        for j in range(REACH):
            shift = bias[s * REACH + j] - top
            at = pl.ds(j * STRETCH, STRETCH)
            value = jnp.exp2((st[at, :] + shift) * (scale * LOG2E))
            st[at, :] = value
            total = total + fold(value, jnp.sum)
        inverse = 1.0 / jnp.sum(total, axis=0, keepdims=True)
        for j in range(REACH):
            at = pl.ds(j * STRETCH, STRETCH)
            wbuf[s, at, :] = (st[at, :] * inverse).astype(jnp.bfloat16)
        contrib_v[pl.ds(s * REACH, REACH)] = dot(wbuf[s], gcat[s], nn).reshape(REACH, STRETCH, HD)

    per = STRETCH // short

    def key_side(s):
        g = gcat[s]
        for j in range(REACH):
            value = vbuf[slots[s * REACH + j]]
            kext[pl.ds(j * STRETCH, STRETCH), :] = value
            kt[:, pl.ds(j * STRETCH, STRETCH)] = value.T
        st[...] = dot(kext[...], g, nt)
        ot = dot(kt[...], wbuf[s], nn).astype(jnp.bfloat16)
        ot = ot.astype(jnp.float32)
        dots = []
        for h in range(4):
            part = ot[:, h * HD:(h + 1) * HD]
            outbuf[s, :, pl.ds(h * HD, HD)] = part.T.astype(jnp.bfloat16)
            gt = g[h * STRETCH:(h + 1) * STRETCH, :].astype(jnp.float32).T
            dots.append(jnp.sum(gt * part, axis=0, keepdims=True))
        dots = jnp.concatenate(dots, axis=1)
        pltpu.make_async_copy(
            outbuf.at[s],
            out_hbm.at[rows(s * STRETCH, STRETCH, STRETCH)], out_sem.at[s],
        ).start()

        for j in range(REACH):
            at = pl.ds(j * STRETCH, STRETCH)
            w = wbuf[s, at, :].astype(jnp.float32)
            wbuf[s, at, :] = (w * (st[at, :] - dots)).astype(jnp.bfloat16)

        contrib_k[pl.ds(s * REACH, REACH)] = (
            dot(wbuf[s], qcat[s], nn) * scale
        ).reshape(REACH, STRETCH, HD)

    def query_side(s):
        for j in range(REACH):
            kt[:, pl.ds(j * STRETCH, STRETCH)] = kbuf[slots[s * REACH + j]].T
        dqt = dot(kt[...], wbuf[s], nn) * scale
        for h in range(4):
            dqbuf[pl.ds(s * per, per), :, pl.ds(h * HD, HD)] = dqt[
                :, h * HD:(h + 1) * HD
            ].T.reshape(per, short, HD).astype(jnp.bfloat16)

        @pl.loop(0, per)
        def _(i):
            b = s * per + i

            def remote():
                dq_copy(b, head, b).start()

            def own():
                dqrecv[head] = dqbuf[b]

            pl.when(b != head)(remote)
            pl.when(b == head)(own)

    def dq_copy(b, src, to):
        return pltpu.make_async_remote_copy(
            src_ref=dqbuf.at[b], dst_ref=dqrecv.at[src],
            send_sem=dq_send.at[b], recv_sem=dq_recv.at[src],
            device_id={"head": to}, device_id_type=pl.DeviceIdType.MESH,
        )

    contribs = (contrib_k, contrib_v)
    parts = (part_k, part_v)
    sibs = (sib_k, sib_v)

    def build(t, at):
        @pl.loop(0, 4)
        def _(k):
            here = order[at * 4 + k]
            total = None
            for s in range(4):
                delta = order[ctx * 4 + s] - here
                index = jnp.where(
                    (delta >= 0) & (delta < REACH), s * REACH + REACH - 1 - delta, 4 * REACH
                )
                term = contribs[t][index]
                total = term if total is None else total + term
            parts[t][at * 4 + k] = total.astype(jnp.bfloat16)

    def rs_copy(t, src, dst_, sem, device):
        return pltpu.make_async_remote_copy(
            src_ref=src, dst_ref=dst_, send_sem=rs_send.at[t, sem], recv_sem=rs_recv.at[t, sem],
            device_id=device, device_id_type=pl.DeviceIdType.MESH,
        )

    def rs_wait(t, ref, sem):
        rs_copy(t, ref, ref, sem, up).wait_recv()

    def dest(i):
        return zmod(z + far + ((i + 1) // 2) * (2 * lax.rem(i, 2) - 1))

    def rs_build(t):
        @pl.loop(0, nz)
        def _(i):
            rs_dest(t, i)

    def rs_dest(t, i):
        zt = dest(i)
        other = zt * 2 + 1 - core
        build(t, other)
        rs_copy(
            t, parts[t].at[pl.ds(other * 4, 4)], sibs[t].at[pl.ds(i * 4, 4)], RS_S + i, sib
        ).start()
        build(t, zt * 2 + core)

    def place(i):
        if i == nz - 1:
            return z
        delta = far + ((i + 1) // 2) * (2 * (i % 2) - 1)
        return zmod(z + delta)

    def chip_sum(t, i, start, size):
        return (
            parts[t][pl.ds((place(i) * 2 + core) * 4 + start, size)].astype(jnp.float32)
            + sibs[t][pl.ds(i * 4 + start, size)].astype(jnp.float32)
        )

    def own_x(t, i):
        rs_wait(t, yrecv.at[t, i], RS_Y + i)
        return chip_sum(t, i, x0, 1)[0] + yrecv[t, i].astype(jnp.float32)

    def own(t, u, i):
        return own_x(t, i) if u == 0 else chip_sum(t, i, u, 1)[0]

    def rs_chain(t, way, u, k):
        sem, first = chain(way, u), far + 1 - hops(way, u)
        c = way * 3 + u
        i = 2 * (k - 1) if way == UP else max(0, 2 * k - 3)
        if k > first:
            rs_wait(t, ring_in.at[t, c, k - 1], sem + k - 2)
        total = own(t, u, i)
        if k > first:
            total = total + ring_in[t, c, k - 1].astype(jnp.float32)
        ring_out[t, c, k] = total.astype(jnp.bfloat16)
        rs_copy(
            t, ring_out.at[t, c, k], ring_in.at[t, c, k], sem + k - 1, (up, down)[way]
        ).start()

    def rs_begin(t):
        for i in range(nz):
            rs_wait(t, sibs[t].at[pl.ds(i * 4, 4)], RS_S + i)
            ysend[t, i] = chip_sum(t, i, ox0, 1)[0].astype(jnp.bfloat16)
            rs_copy(t, ysend.at[t, i], yrecv.at[t, i], RS_Y + i, partner).start()
            if i == 0:
                rs_chain(t, DOWN, 1, 1)
                rs_chain(t, DOWN, 2, 1)
            if i == 2:
                rs_chain(t, UP, 1, 2)
                rs_chain(t, UP, 2, 2)

    def rs_begin_x(t):
        rs_chain(t, UP, 0, 1)
        rs_chain(t, DOWN, 0, 2)

    def rs_step(t, k):
        for way, u in ORDER[:1] + ORDER[2:] + ORDER[1:2]:
            if k > far + 1 - hops(way, u):
                rs_chain(t, way, u, k)

    b0 = par * (XROWS // short)
    nb = ring_rows // short
    own_in = (head >= b0) & (head < b0 + nb)

    def fin_copy(t, b, src, u=0, i=0):
        return pltpu.make_async_remote_copy(
            src_ref=fin.at[t, u, pl.ds(i * short, short)], dst_ref=finrecv.at[t, src],
            send_sem=fin_send.at[t, b], recv_sem=fin_recv.at[t, src],
            device_id={"head": b}, device_id_type=pl.DeviceIdType.MESH,
        )

    def rs_final(t):
        for u in (1, 2, 0):
            total = own(t, u, nz - 1)
            for way in (UP, DOWN):
                c = way * 3 + u
                rs_wait(t, ring_in.at[t, c, far], chain(way, u) + far - 1)
                total = total + ring_in[t, c, far].astype(jnp.float32)
            fin[t, u] = total.astype(jnp.bfloat16)
            for i in range(per):
                b = at_unit(u) * per + i

                def keep(u=u, i=i):
                    finrecv[t, head] = fin[t, u, pl.ds(i * short, short), :]

                pl.when(b != head)(lambda u=u, i=i, b=b: fin_copy(t, b, head, u, i).start())
                pl.when(b == head)(keep)

    def rs_out(t, ref):
        @pl.loop(0, nh)
        def _(src):
            p = lax.rem(src, 2)
            sends = ((p == 0) & (head < last_b)) | ((p == 1) & (head >= first_b))
            pl.when(sends & (src != head))(lambda: fin_copy(t, 0, src).wait_recv())

        for g in range(nh // 2):
            ref[:, g * HD:(g + 1) * HD] = (
                finrecv[t, 2 * g].astype(jnp.float32) + finrecv[t, 2 * g + 1].astype(jnp.float32)
            ).astype(jnp.bfloat16)

    ag_first(0)
    ag_first(1)
    ag_step(0, 1)
    ag_step(1, 1)
    ag_step(0, 2)
    ag_step(1, 2)
    ag_step(0, 3)
    ag_step(1, 3)
    ag_step(0, 4)
    ag_finish(0)
    for n, s, h in heads:
        load_qg(n, s, h).wait()

    @pl.loop(0, 4)
    def _(s):
        scores(s)
        pl.when(s < far - 3)(lambda: ag_half(1, s + 4, 0))
        softmax(s)
        pl.when(s < far - 3)(lambda: ag_half(1, s + 4, 1))

    rs_build(1)
    ag_finish(1)
    key_side(0)
    rs_begin(1)
    key_side(1)
    key_side(2)
    key_side(3)
    rs_build(0)
    rs_begin_x(1)
    rs_begin(0)
    rs_step(1, 2)
    query_side(0)
    rs_begin_x(0)
    rs_step(1, 3)
    query_side(1)
    rs_step(0, 2)
    rs_step(1, 4)
    query_side(2)
    rs_step(0, 3)
    rs_final(1)
    query_side(3)
    rs_step(0, 4)
    rs_out(1, dv_ref)
    rs_final(0)

    @pl.loop(0, nh)
    def _(src):
        pl.when(src != head)(lambda: dq_copy(0, src, src).wait_recv())

    for src in range(nh):
        dq_ref[:, src * 4 * HD:(src + 1) * 4 * HD] = dqrecv[src]
    @pl.loop(0, nh)
    def _(b):
        pl.when(b != head)(lambda: dq_copy(b, head, b).wait_send())

    for s in range(4):
        pltpu.make_async_copy(
            outbuf.at[s], out_hbm.at[pl.ds(s * STRETCH, STRETCH)], out_sem.at[s]
        ).wait()
    for t in range(2):
        chains = [(chain(w, u) + far - hops(w, u), hops(w, u)) for w, u in ORDER]
        for first, count, size in [(chain(w, u), hops(w, u), 1) for w, u in ORDER] + [
            (AG_Y, far, 1), (AG_Y + 4, far - 1, 1), (AG_SR, nz, 3), (AG_SO, nz, 1),
        ]:

            @pl.loop(first, first + count)
            def _(sem):
                ag_copy(t, z, 0, size, sem, up).wait_send()

        for first, count, ref in [(f, n, yrecv.at[t, 0]) for f, n in chains] + [
            (RS_S, nz, sibs[t].at[pl.ds(0, 4)]), (RS_Y, nz, yrecv.at[t, 0]),
        ]:

            @pl.loop(first, first + count)
            def _(sem):
                rs_copy(t, ref, ref, sem, up).wait_send()

        @pl.loop(0, nb)
        def _(i):
            pl.when(b0 + i != head)(lambda: fin_copy(t, b0 + i, head).wait_send())

    rs_out(0, dk_ref)


def on_device(query_states, key_states, value_states, out_grad, stretch_order, doc_blocks):
    nz = lax.axis_size("ctx") // 2
    nh = lax.axis_size("head")
    far = nz // 2
    local = 4 * STRETCH
    crows = local - 2 * XROWS
    short = local // nh
    seq = 2 * nz * local
    bf, f32 = jnp.bfloat16, jnp.float32
    anywhere = pl.BlockSpec(memory_space=pl.ANY)
    smem = pl.BlockSpec(memory_space=pltpu.SMEM)
    vmem = pl.BlockSpec(memory_space=pltpu.VMEM)
    V, D = pltpu.VMEM, pltpu.SemaphoreType.DMA
    results = pl.pallas_call(
        functools.partial(kernel, nz, nh),
        out_shape=(
            jax.ShapeDtypeStruct((local, 4 * HD), bf),
            jax.ShapeDtypeStruct((short, nh * 4 * HD), bf),
            jax.ShapeDtypeStruct((short, nh // 2 * HD), bf),
            jax.ShapeDtypeStruct((short, nh // 2 * HD), bf),
        ),
        in_specs=[smem, smem, anywhere, anywhere, anywhere, anywhere],
        out_specs=(anywhere, vmem, vmem, vmem),
        scratch_shapes=[
            V((seq // STRETCH, STRETCH, HD), bf), V((seq // STRETCH, STRETCH, HD), bf),
            V((4, 512, HD), bf), V((4, 512, HD), bf),
            V((1024, HD), bf), V((HD, 1024), bf),
            V((1024, 512), f32), V((4, 1024, 512), bf), V((1, 512), f32),
            V((4 * REACH + 1, STRETCH, HD), f32), V((4 * REACH + 1, STRETCH, HD), f32),
            V((seq // STRETCH, STRETCH, HD), bf), V((seq // STRETCH, STRETCH, HD), bf),
            V((nz * 4, STRETCH, HD), bf), V((nz * 4, STRETCH, HD), bf),
            V((2, nz, XROWS, HD), bf), V((2, nz, XROWS, HD), bf),
            V((2, 6, far + 1, STRETCH, HD), bf), V((2, 6, far + 1, STRETCH, HD), bf),
            V((2, 3, STRETCH, HD), bf), V((2, nh, short, HD), bf),
            V((4, STRETCH, 4 * HD), bf), V((nh, short, 4 * HD), bf), V((nh, short, 4 * HD), bf),
            pltpu.SMEM((4 * REACH,), jnp.int32), pltpu.SMEM((4 * REACH,), f32),
            D((2, AG_N)), D((2, AG_N)), D((2, RS_N)), D((2, RS_N)),
            D((2, nh)), D((2, nh)), D((nh,)), D((nh,)), D((4, 16)), D((4,)),
        ],
        compiler_params=pltpu.CompilerParams(
            collective_id=0, has_side_effects=True, vmem_limit_bytes=56 * 1024 * 1024
        ),
        cost_estimate=pl.CostEstimate(
            flops=3_300_000_000, bytes_accessed=4_000_000, transcendentals=2_100_000
        ),
    )(stretch_order, doc_blocks, query_states, key_states, value_states, out_grad)
    return pl.pallas_call(
        settle,
        out_shape=tuple(jax.ShapeDtypeStruct(r.shape, r.dtype) for r in results),
        in_specs=[vmem] * 4,
        out_specs=(vmem,) * 4,
    )(*results)


def settle(*refs):
    for n in range(4):
        refs[4 + n][...] = refs[n][...]


def solution(mesh):
    in_specs = (P("ctx", "head"), P("ctx", None), P("ctx", None), P("ctx", "head"), P(), P())
    out_specs = (
        P("ctx", "head"),
        P(("ctx", "head"), None),
        P(("ctx", "head"), None),
        P(("ctx", "head"), None),
    )
    return jax.shard_map(
        on_device, mesh=mesh, in_specs=in_specs, out_specs=out_specs, check_vma=False
    )
```
